512 devices in a mesh: rad: 8 (over y), ang: 64 (over x, z, core).
Axes of the slice: x: 4, y: 8, z: 8, core: 2. Of those that a mesh axis runs over, the one named last changes fastest.
Arguments:
- state: bfloat16 [6, 2, 1024, 256, 128], P(None, None, ('rad', 'ang')), may hold values from -6 to 6
- legendre: bfloat16 [1024, 192, 256], P(('rad', 'ang')), may hold values from -0.375 to 0.375
- radial_ops: bfloat16 [2, 128, 256], replicated, may hold values from -0.375 to 0.375
- base_flow: bfloat16 [3, 384, 128, 1024], P(None, 'ang', 'rad'), may hold values from -6 to 6
- base_field: bfloat16 [3, 384, 128, 1024], P(None, 'ang', 'rad'), may hold values from -6 to 6
- assign: int32 [512, 2], replicated, may hold values from -1 to 511, as said below
- counts: int32 [512], replicated, may hold values from 0 to 2, as said below
Outputs:
- tangent: bfloat16 [6, 2, 1024, 256, 128], P(None, None, ('rad', 'ang'))
The draws below stay inside these ranges and needn't reach their ends.
Inputs may be any that keep to these rules, and one draw needn't show every extreme that they name: Slot j of device d (d = the rad index times the ang axis's size plus the ang index) holds order assign[d, j] when j < counts[d] and -1 otherwise; each order 0 to 511 is held by exactly one live slot. counts[d] plus the count of the device with the same rad index whose ang index differs by half the ang axis equals 2.
All inputs are finite; a program needn't handle non-finite values.
Results may differ from the reference program's by a relative error of at most 0.01.
Values may be sent and summed in bfloat16 or wider, within the bound.
A program may use at most 128 MiB of HBM per device.

```python
import math
import jax
import jax.numpy as jnp
from jax import lax

ND = 256
R = 128
NLAT_H = 192
NPHI = 1024
STEPS = 1
MW = 512
CAP = 2
SLOTS = 1024
NLAT = 384
N_RAD = 8
N_ANG = 64
DEVICES = 512


def placement_draw(key):
    half_axis = N_ANG // 2
    lower = jax.random.randint(jax.random.fold_in(key, 101), (N_RAD, half_axis), 0, CAP + 1)
    lower = lower.at[0, 0].set(CAP)
    held = jnp.concatenate([lower, CAP - lower], axis=1).reshape(DEVICES).astype(jnp.int32)
    shuffled = jax.random.permutation(jax.random.fold_in(key, 102), MW).astype(jnp.int32)
    offsets = jnp.cumsum(held) - held
    slot_idx = jnp.arange(CAP, dtype=jnp.int32)
    position = jnp.clip(offsets[:, None] + slot_idx[None, :], 0, MW - 1)
    is_live = slot_idx[None, :] < held[:, None]
    return (held, jnp.where(is_live, shuffled[position], -1).astype(jnp.int32))


def draw_assign(key, part):
    shared = placement_draw(key)
    return shared[1]


def draw_counts(key, part):
    shared = placement_draw(key)
    return shared[0]


def levels(rng, extent, pieces, low, top_value):
    loudness, own = 1.0, jax.random.fold_in(rng, 6)
    for axis_at, blocks in pieces:
        draws = jnp.exp(jax.random.uniform(jax.random.fold_in(own, axis_at), (blocks,), jnp.float32, low / len(pieces), top_value / len(pieces)))
        loudness = loudness * jnp.repeat(draws, extent[axis_at] // blocks).reshape([-1 if axis == axis_at else 1 for axis in range(len(extent))])
    return loudness


def centred(own_key, shape, scale, reach, split=(), held_as=jnp.bfloat16):
    factor_of = levels(own_key, shape, split, -0.22, 0.18) if split else 1.0
    array = jax.random.normal(own_key, shape, jnp.float32) * scale * factor_of
    return jnp.minimum(jnp.maximum(array, -reach), reach).astype(held_as)


def setup_inputs(seed: int = 0) -> dict:
    seeds = jax.random.split(jax.random.key(seed), 8)
    return {
        "state": centred(seeds[0], (6, 2, SLOTS, ND, R), 1.0, 6.0, ((2, 512),)),
        "legendre": centred(seeds[1], (SLOTS, NLAT_H, ND), ND ** -0.5, 0.375, ((0, 512),)),
        "radial_ops": centred(seeds[2], (2, R, 2 * R), (2 * R) ** -0.5, 0.375),
        "base_flow": centred(seeds[3], (3, NLAT, R, NPHI), 1.0, 6.0, ((1, 64), (2, 8))),
        "base_field": centred(seeds[4], (3, NLAT, R, NPHI), 1.0, 6.0, ((1, 64), (2, 8))),
        "assign": draw_assign(jax.random.fold_in(seeds[7], 71), 0),
        "counts": draw_counts(jax.random.fold_in(seeds[7], 71), 0),
    }


coriolis = 3.0

def cross_product(first_vec, second_vec):
    return jnp.stack([first_vec[1] * second_vec[2] - first_vec[2] * second_vec[1], first_vec[2] * second_vec[0] - first_vec[0] * second_vec[2], first_vec[0] * second_vec[1] - first_vec[1] * second_vec[0]])

def trig_table(orders, points, factor):
    positions = jnp.arange(points, dtype=jnp.int32)
    wrapped = orders[:, None] * positions[None, :] % points
    angles = wrapped.astype(jnp.float32) * (2.0 * math.pi / points)
    stacked = jnp.stack([jnp.cos(angles), -jnp.sin(angles)]) * factor[None, :, None]
    return stacked.astype(jnp.bfloat16)

def colatitude(row_index, lat_rows):
    northern = ((row_index // 2).astype(jnp.float32) + 0.5) * (math.pi / lat_rows)
    return jnp.where(row_index % 2 == 1, math.pi - northern, northern)

def reference(state, legendre, radial_ops, base_flow, base_field, assign, counts):
    is_live = jnp.arange(CAP, dtype=jnp.int32)[None, :] < counts[:, None]
    orders = jnp.where(is_live, assign, 0).reshape(-1).astype(jnp.int32)
    is_live = is_live.reshape(-1)
    degree_idx = jnp.arange(ND, dtype=jnp.int32)
    usable = is_live[:, None] & (orders[:, None] + degree_idx[None, :] < MW)
    masked_rows = legendre * usable[:, None, :].astype(jnp.bfloat16)
    degree_sum = (orders[:, None] + degree_idx[None, :]).astype(jnp.float32)
    damping = jnp.where(usable, 1.0 / (1.0 + degree_sum * (degree_sum + 1.0) / (ND * ND)), 0.0).astype(jnp.float32)
    synth_table = trig_table(orders, NPHI, jnp.full((SLOTS,), 1.0 / math.sqrt(MW), jnp.float32)).astype(jnp.float32)
    anal_factor = jnp.where(orders == 0, 1.0, 2.0).astype(jnp.float32) * (math.sqrt(MW) / NPHI)
    anal_table = trig_table(orders, NPHI, anal_factor).astype(jnp.float32)
    colat_rows = colatitude(jnp.arange(NLAT, dtype=jnp.int32), NLAT)
    operators = radial_ops.astype(jnp.float32)
    current = state
    for repeat in range(STEPS):

        def synth_slot(slot_index):
            coeffs = lax.dynamic_index_in_dim(current, slot_index, axis=2, keepdims=False).astype(jnp.float32)
            row_vals = lax.dynamic_index_in_dim(masked_rows, slot_index, axis=0, keepdims=False).astype(jnp.float32)
            even_part = jnp.einsum('cxnr,tn->cxtr', coeffs[:, :, 0::2], row_vals[:, 0::2])
            odd_part = jnp.einsum('cxnr,tn->cxtr', coeffs[:, :, 1::2], row_vals[:, 1::2])
            joined = jnp.stack([even_part + odd_part, even_part - odd_part], axis=3)
            return joined.reshape(6, 2, NLAT, R).astype(jnp.bfloat16)
        grid_vals = lax.map(synth_slot, jnp.arange(SLOTS, dtype=jnp.int32))

        def grid_row(row_index):
            values = lax.dynamic_index_in_dim(grid_vals, row_index, axis=3, keepdims=False).astype(jnp.float32)
            fields = jnp.einsum('scxr,xsk->crk', values, synth_table)
            base_vel = lax.dynamic_index_in_dim(base_flow, row_index, axis=1, keepdims=False).astype(jnp.float32)
            magnet = lax.dynamic_index_in_dim(base_field, row_index, axis=1, keepdims=False).astype(jnp.float32)
            angle_row = colat_rows[row_index]
            axis_dir = jnp.stack([jnp.cos(angle_row), -jnp.sin(angle_row), jnp.zeros_like(angle_row)])[:, None, None]
            spin_axis = base_vel + coriolis * axis_dir
            momentum = cross_product(fields[:3], spin_axis) + cross_product(magnet, fields[3:])
            induction = cross_product(fields[:3], magnet) + cross_product(base_vel, fields[3:])
            weight = math.pi / 2 * jnp.sin(angle_row)
            products = (jnp.concatenate([momentum, induction]) * weight).astype(jnp.bfloat16)
            products = lax.optimization_barrier(products).astype(jnp.float32)
            return jnp.einsum('crk,xsk->scxr', products, anal_table).astype(jnp.bfloat16)
        returned = lax.map(grid_row, jnp.arange(NLAT, dtype=jnp.int32))

        def finish_slot(slot_index):
            row_vals = lax.dynamic_index_in_dim(returned, slot_index, axis=1, keepdims=False).astype(jnp.float32)
            row_vals = row_vals.reshape(NLAT_H, 2, 6, 2, R)
            hemi_sum = lax.optimization_barrier((row_vals[:, 0] + row_vals[:, 1]).astype(jnp.bfloat16)).astype(jnp.float32)
            hemi_diff = lax.optimization_barrier((row_vals[:, 0] - row_vals[:, 1]).astype(jnp.bfloat16)).astype(jnp.float32)
            slot_rows = lax.dynamic_index_in_dim(masked_rows, slot_index, axis=0, keepdims=False).astype(jnp.float32)
            coef_even = jnp.einsum('tcxr,tn->cxnr', hemi_sum, slot_rows[:, 0::2])
            coef_odd = jnp.einsum('tcxr,tn->cxnr', hemi_diff, slot_rows[:, 1::2])
            nonlinear = jnp.stack([coef_even, coef_odd], axis=3).reshape(6, 2, ND, R).astype(jnp.bfloat16)
            nonlinear = lax.optimization_barrier(nonlinear)
            coeffs = lax.dynamic_index_in_dim(current, slot_index, axis=2, keepdims=False)
            joined = jnp.concatenate([coeffs, nonlinear], axis=-1).astype(jnp.float32).reshape(2, 3, 2, ND, 2 * R)
            stepped = jnp.einsum('fkxnq,frq->fkxnr', joined, operators).reshape(6, 2, ND, R)
            scaling = lax.dynamic_index_in_dim(damping, slot_index, axis=0, keepdims=False)
            return (stepped * scaling[None, None, :, None]).astype(jnp.bfloat16)
        result = lax.map(finish_slot, jnp.arange(SLOTS, dtype=jnp.int32))
        current = jnp.moveaxis(result, 0, 2)
    return current
```

```python
import functools
import math

import jax
import jax.numpy as jnp
from jax import lax
from jax.experimental import pallas as pl
from jax.experimental.pallas import tpu as pltpu
from jax.sharding import PartitionSpec as P

F32 = jnp.float32
BF16 = jnp.bfloat16
MESH = pl.DeviceIdType.MESH

NX = 4
NZ = 16
NY = 8
NC = 3
NG = 3
STAGES = 6
coriolis = 3.0


def iota(shape, axis):
    return lax.broadcasted_iota(jnp.int32, shape, axis)


def dot(a, b, dims=((1,), (0,))):
    return lax.dot_general(a, b, (dims, ((), ())), preferred_element_type=F32)


def kernel(
    assign_ref,
    counts_ref,
    pair_ref,
    state_ref,
    leg_ref,
    ops_ref,
    flow_ref,
    mag_ref,
    out_ref,
    swap,
    turn,
    leg_fwd,
    leg_back,
    coeffs,
    table,
    table_back,
    lhs,
    fields,
    prods,
    xs,
    xr,
    ys,
    yr,
    zs,
    zr,
    zbs,
    zbr,
    ybs,
    ybr,
    xbr,
    xsem,
    ysem,
    zsem,
    zbsem,
    ybsem,
    xbsem,
    lsem,
):
    my = lax.axis_index("rad")
    ang = lax.axis_index("ang")
    mx = ang // NZ
    mz = ang % NZ
    upper = mx // 2
    device = my * (NX * NZ) + ang

    def at_x(x):
        return (my, x * NZ + mz)

    def at_y(y):
        return (y, ang)

    def at_z(z):
        return (my, mx * NZ + z)

    barrier = pltpu.get_barrier_semaphore()

    @pl.loop(1, NX)
    def _(d):
        pl.semaphore_signal(barrier, inc=1, device_id=at_x((mx + d) % NX), device_id_type=MESH)

    @pl.loop(1, NY)
    def _(d):
        pl.semaphore_signal(barrier, inc=1, device_id=at_y((my + d) % NY), device_id_type=MESH)

    @pl.loop(1, NZ)
    def _(d):
        pl.semaphore_signal(barrier, inc=1, device_id=at_z((mz + d) % NZ), device_id_type=MESH)

    def remote(src, dst, sems, i, d, target):
        return pltpu.make_async_remote_copy(
            src_ref=src,
            dst_ref=dst,
            send_sem=sems.at[0, i, d],
            recv_sem=sems.at[1, i, d],
            device_id=target,
            device_id_type=MESH,
        )

    def x_copy(i, d):
        x = (mx + d) % NX
        return remote(xs.at[i, x], xr.at[i, mx], xsem, i, d, at_x(x))

    def y_copy(i, d):
        y = (my + d) % NY
        return remote(ys.at[i, y], yr.at[i, my], ysem, i, d, at_y(y))

    def z_copy(i, d):
        z = (mz + d) % NZ
        return remote(zs.at[i, z], zr.at[i, mz], zsem, i, d, at_z(z))

    def zb_copy(i, d):
        z = (mz + d) % NZ
        return remote(zbs.at[i, z], zbr.at[i, mz], zbsem, i, d, at_z(z))

    def yb_copy(i, d):
        y = (my + d) % NY
        return remote(ybs.at[i, y], ybr.at[i, my], ybsem, i, d, at_y(y))

    def xb_copy(i, d):
        x = (mx + d) % NX
        return remote(ybr.at[i, :, x % 2], xbr.at[i, mx], xbsem, i, d, at_x(x))

    def own(k, i):
        src, dst = (
            (xs.at[i, mx], xr.at[i, mx]),
            (ys.at[i, my], yr.at[i, my]),
            (zs.at[i, mz], zr.at[i, mz]),
            (zbs.at[i, mz], zbr.at[i, mz]),
            (ybs.at[i, my], ybr.at[i, my]),
            (ybr.at[i, :, mx % 2], xbr.at[i, mx]),
        )[k]
        return pltpu.make_async_copy(src, dst, lsem.at[k, i])

    copies = (x_copy, y_copy, z_copy, zb_copy, yb_copy, xb_copy)
    sizes = (NX, NY, NZ, NZ, NY, NX)

    def send(k, i):
        own(k, i).start()

        @pl.loop(1, sizes[k])
        def _(d):
            copies[k](i, d).start()

    def receive(k, i):
        @pl.loop(1, sizes[k])
        def _(d):
            copies[k](i, d).wait_recv()

        own(k, i).wait()

    def slot(pos):
        return (1 - upper) * pos + upper * (1 - pos)

    @pl.loop(0, 4)
    def _(b):
        row = iota((256, 1024), 0) + b * 256
        col = iota((256, 1024), 1)
        image = (row % 128) // 16 * 128 + row // 128 * 16 + row % 16
        swap[pl.ds(pl.multiple_of(b * 256, 256), 256), :] = jnp.where(col == image, 1.0, 0.0).astype(BF16)

    def masks(pos):
        s = slot(pos)
        live = s < counts_ref[device]
        order = jnp.where(live, assign_ref[device * 2 + s], 0)
        top = jnp.where(live, 511 - order, -1)
        return order, top

    for pos in range(2):
        _, top = masks(pos)
        rows = leg_ref[slot(pos)]
        rows = jnp.where(iota((192, 256), 1) <= top, rows.astype(F32), 0.0).astype(BF16)
        for i in range(NC):
            r = iota((128, 192), 0)
            pick = jnp.where(iota((128, 192), 1) == 3 * (r // 32 * 16 + r % 16) + i, 1.0, 0.0).astype(BF16)
            picked = dot(pick, rows)
            odd_n = iota((128, 256), 1) % 2
            south = iota((128, 256), 0) // 16 % 2
            leg_fwd[i, pos * 128 : (pos + 1) * 128, :] = jnp.where(odd_n * south == 1, -picked, picked).astype(BF16)
            kept = jnp.where(odd_n == south, picked, 0.0)
            leg_back[pos, :, i * 128 : (i + 1) * 128] = kept.T.astype(BF16)

    for g in range(NG):
        joined = jnp.concatenate(
            [state_ref[2 * g + cc, x, slot(pos)] for pos in range(2) for x in range(2) for cc in range(2)], axis=1
        )
        for b in range(4):
            coeffs[g, :, b * 256 : (b + 1) * 256] = dot(joined, swap[:, b * 256 : (b + 1) * 256]).astype(BF16)

    first = iota((128, 256), 1) % 128 < 64

    def synthesis(i):
        @pl.loop(0, NG)
        def _(g):
            for b in range(4):
                both = dot(leg_fwd[i], coeffs[g, :, b * 256 : (b + 1) * 256])
                grid = jnp.where(first, both[:128], both[128:]).astype(BF16)
                xs[i, :, g, :, b * 256 : (b + 1) * 256] = grid.reshape(NX, 32, 256)

    synthesis(0)
    pl.semaphore_wait(barrier, NX + NY + NZ - 3)
    send(0, 0)

    @pl.loop(1, NC)
    def _(i):
        synthesis(i)
        send(0, i)

    a = iota((512, 512), 0)
    b = iota((512, 512), 1)
    image = (a % 16) * 32 + a // 16 % 2 * 16 + a // 32
    turn[...] = jnp.where(b == image, 1.0, 0.0).astype(BF16)

    scale = 1.0 / math.sqrt(512)
    for pos in range(2):
        m = pair_ref[:, pos : pos + 1]
        lane = iota((256, 128), 1)
        fine = (m * lane & 1023).astype(F32) * (2.0 * math.pi / 1024)
        cos_fine = jnp.cos(fine) * scale
        sin_fine = jnp.sin(fine) * scale
        coarse = (m * lane & 7).astype(F32) * (2.0 * math.pi / 8)
        cos_coarse = jnp.cos(coarse)
        sin_coarse = jnp.sin(coarse)
        back = jnp.where(m == 0, 0.5, 1.0)
        for k in range(8):
            ck = cos_coarse[:, k : k + 1]
            sk = sin_coarse[:, k : k + 1]
            re = (cos_fine * ck - sin_fine * sk).astype(BF16)
            im = (-(sin_fine * ck + cos_fine * sk)).astype(BF16)
            lanes = slice(k * 128, (k + 1) * 128)
            table[pos * 512 : pos * 512 + 256, lanes] = re
            table[pos * 512 + 256 : pos * 512 + 512, lanes] = im
            table_back[pos * 512 : pos * 512 + 256, lanes] = (re.astype(F32) * back).astype(BF16)
            table_back[pos * 512 + 256 : pos * 512 + 512, lanes] = (im.astype(F32) * back).astype(BF16)

    def fold(i):
        receive(0, i)
        for p in range(2):
            for g in range(NG):
                pair = xr[i, p, g] + xr[i, p + 2, g]
                for y in range(NY):
                    ys[i, y, g, p] = pair[:, y * 128 : (y + 1) * 128]
        send(1, i)

    def spread(i):
        receive(1, i)
        rows = jnp.concatenate([yr[i, :, g].reshape(512, 128) for g in range(NG)], axis=1)
        turned = dot(turn[...], rows).astype(BF16)
        for g in range(NG):
            zs[i, :, g] = turned[:, g * 128 : (g + 1) * 128].reshape(NZ, 32, 128)
        send(2, i)

    def physics(i):
        receive(2, i)
        for g in range(NG):
            for h in range(2):
                block = zr[i, :, g, h * 16 : (h + 1) * 16, :].reshape(256, 128).T
                for p in range(4):
                    row = h * 96 + g * 32
                    lhs[row : row + 32, p * 256 : (p + 1) * 256] = block[p * 32 : (p + 1) * 32]

        @pl.loop(0, 4)
        def _(b):
            lanes = pl.ds(pl.multiple_of(b * 256, 256), 256)
            fields[:, lanes] = dot(lhs[...], table[:, lanes])

        row_t = (iota((8, 128), 0) * 0 + ang * NC + i).astype(F32)
        north = (row_t + 0.5) * (math.pi / 384)
        for h in range(2):
            colat = math.pi - north if h == 1 else north
            along = (coriolis * jnp.cos(colat))[0:1, 0:1]
            across = (-coriolis * jnp.sin(colat))[0:1, 0:1]
            weight = (math.pi / 2 * jnp.sin(colat))[0:1, 0:1]

            @pl.loop(0, 4)
            def _(b):
                lanes = pl.ds(pl.multiple_of(b * 256, 256), 256)
                u = [fields[h * 96 + c * 16 : h * 96 + (c + 1) * 16, lanes] for c in range(3)]
                v = [fields[h * 96 + (c + 3) * 16 : h * 96 + (c + 4) * 16, lanes] for c in range(3)]
                w = [flow_ref[c, 2 * i + h, :, lanes].astype(F32) for c in range(3)]
                f = [mag_ref[c, 2 * i + h, :, lanes].astype(F32) for c in range(3)]
                spin = [w[0] + along, w[1] + across, w[2]]
                for c in range(3):
                    n, o = (c + 1) % 3, (c + 2) % 3
                    momentum = (u[n] * spin[o] - u[o] * spin[n]) + (f[n] * v[o] - f[o] * v[n])
                    induction = (u[n] * f[o] - u[o] * f[n]) + (w[n] * v[o] - w[o] * v[n])
                    row = h * 96 + c * 16
                    prods[row : row + 16, lanes] = (momentum * weight).astype(BF16)
                    prods[row + 48 : row + 64, lanes] = (induction * weight).astype(BF16)

        @pl.loop(0, 4)
        def _(p):
            returned = dot(prods[...], table_back[pl.ds(pl.multiple_of(p * 256, 256), 256), :], ((1,), (1,)))
            returned = returned.astype(BF16).astype(F32)
            n, s = returned[:96], returned[96:]
            fields[0:96, pl.ds(pl.multiple_of(p * 256, 256), 256)] = n + s
            fields[96:192, pl.ds(pl.multiple_of(p * 256, 256), 256)] = n - s

        for g in range(NG):
            for h in range(2):
                row = h * 96 + g * 32
                block = jnp.concatenate([fields[row : row + 32, p * 256 : (p + 1) * 256] for p in range(4)], axis=0)
                zbs[i, :, g, h * 16 : (h + 1) * 16, :] = block.T.astype(BF16).reshape(NZ, 16, 128)
        send(3, i)

    def gather(i):
        receive(3, i)
        rows = jnp.concatenate([zbr[i, :, g].reshape(512, 128) for g in range(NG)], axis=1)
        turned = dot(turn[...], rows).astype(BF16)
        for g in range(NG):
            block = turned[:, g * 128 : (g + 1) * 128].reshape(NY, 2, 32, 128)
            for p in range(2):
                ybs[i, :, p, g] = block[:, p]
        send(4, i)

    def unfold(i):
        receive(4, i)
        send(5, i)

    stages = (fold, spread, physics, gather, unfold, functools.partial(receive, 5))

    @pl.loop(0, NC + STAGES - 1)
    def _(step):
        for k, stage in enumerate(stages):

            @pl.when(jnp.logical_and(step >= k, step < k + NC))
            def _():
                stage(step - k)

    @pl.loop(0, NG)
    def _(g):
        halves = []
        for b in range(4):
            rows = jnp.concatenate([xbr[:, :, 2 * b + e, g].reshape(384, 128) for e in range(2)], axis=1)
            halves.append(jnp.where(iota((256, 256), 1) % 128 < 64, dot(leg_back[0], rows), dot(leg_back[1], rows)).astype(BF16))
        nonlinear = jnp.concatenate(halves, axis=1)
        for pos in range(2):
            order, top = masks(pos)
            n = iota((256, 128), 0)
            degree = (order + n).astype(F32)
            damping = jnp.where(n <= top, 1.0 / (1.0 + degree * (degree + 1.0) / 65536.0), 0.0)
            for x in range(2):
                j = pos * 4 + x * 2
                terms = dot(nonlinear, swap[:, j * 128 : (j + 2) * 128]).astype(BF16)
                for cc in range(2):
                    c = 2 * g + cc
                    joined = jnp.concatenate([state_ref[c, x, slot(pos)], terms[:, cc * 128 : (cc + 1) * 128]], axis=1)
                    stepped = dot(joined, ops_ref[c // 3], ((1,), (1,)))
                    out_ref[c, x, slot(pos)] = (stepped * damping).astype(BF16)

    for k in range(STAGES):

        @pl.loop(0, NC)
        def _(i):
            @pl.loop(1, sizes[k])
            def _(d):
                copies[k](i, d).wait_send()


def per_device(state, legendre, radial_ops, base_flow, base_field, assign, counts):
    live = jnp.arange(2, dtype=jnp.int32)[None, :] < counts[:, None]
    orders = jnp.where(live, assign, 0).reshape(NY, 2, 2, NZ, 2)
    pairs = orders[:, 0] + orders[:, 1, :, :, ::-1]
    pairs = jnp.transpose(pairs, (2, 0, 1, 3)).reshape(256, 2)
    vmem = pl.BlockSpec(memory_space=pltpu.VMEM)
    smem = pl.BlockSpec(memory_space=pltpu.SMEM)
    dma = pltpu.SemaphoreType.DMA
    return pl.pallas_call(
        kernel,
        out_shape=jax.ShapeDtypeStruct(state.shape, BF16),
        in_specs=[smem, smem] + [vmem] * 6,
        out_specs=vmem,
        scratch_shapes=[
            pltpu.VMEM((1024, 1024), BF16),
            pltpu.VMEM((512, 512), BF16),
            pltpu.VMEM((NC, 256, 256), BF16),
            pltpu.VMEM((2, 256, 384), BF16),
            pltpu.VMEM((NG, 256, 1024), BF16),
            pltpu.VMEM((1024, 1024), BF16),
            pltpu.VMEM((1024, 1024), BF16),
            pltpu.VMEM((192, 1024), BF16),
            pltpu.VMEM((192, 1024), F32),
            pltpu.VMEM((192, 1024), BF16),
            pltpu.VMEM((NC, NX, NG, 32, 1024), BF16),
            pltpu.VMEM((NC, NX, NG, 32, 1024), BF16),
            pltpu.VMEM((NC, NY, NG, 2, 32, 128), BF16),
            pltpu.VMEM((NC, NY, NG, 2, 32, 128), BF16),
            pltpu.VMEM((NC, NZ, NG, 32, 128), BF16),
            pltpu.VMEM((NC, NZ, NG, 32, 128), BF16),
            pltpu.VMEM((NC, NZ, NG, 32, 128), BF16),
            pltpu.VMEM((NC, NZ, NG, 32, 128), BF16),
            pltpu.VMEM((NC, NY, 2, NG, 32, 128), BF16),
            pltpu.VMEM((NC, NY, 2, NG, 32, 128), BF16),
            pltpu.VMEM((NC, NX, NY, NG, 32, 128), BF16),
            dma((2, NC, NX)),
            dma((2, NC, NY)),
            dma((2, NC, NZ)),
            dma((2, NC, NZ)),
            dma((2, NC, NY)),
            dma((2, NC, NX)),
            dma((STAGES, NC)),
        ],
        compiler_params=pltpu.CompilerParams(
            collective_id=0, has_side_effects=True, vmem_limit_bytes=56 * 1024 * 1024
        ),
    )(assign.reshape(-1), counts, pairs, state, legendre, radial_ops, base_flow, base_field)


def solution(mesh):
    placed = (
        P(None, None, ("rad", "ang"), None, None),
        P(("rad", "ang"), None, None),
        P(),
        P(None, "ang", "rad", None),
        P(None, "ang", "rad", None),
        P(),
        P(),
    )
    return jax.shard_map(
        per_device,
        mesh=mesh,
        in_specs=placed,
        out_specs=P(None, None, ("rad", "ang"), None, None),
        check_vma=False,
    )
```

```python
import math

import jax
import jax.numpy as jnp
from jax import lax
from jax.experimental import pallas as pl
from jax.experimental.pallas import tpu as pltpu
from jax.sharding import PartitionSpec as P

F32 = jnp.float32
BF16 = jnp.bfloat16
MESH = pl.DeviceIdType.MESH

NX = 4
NZ = 16
NY = 8
NC = 3
NG = 3
NQ = NC * NG
coriolis = 3.0


def iota(shape, axis):
    return lax.broadcasted_iota(jnp.int32, shape, axis)


def dot(a, b, dims=((1,), (0,))):
    return lax.dot_general(a, b, (dims, ((), ())), preferred_element_type=F32)


def kernel(
    assign_ref,
    counts_ref,
    assign_rows_ref,
    counts_row_ref,
    leg_ref,
    ops_ref,
    state_ref,
    flow_ref,
    mag_ref,
    out_ref,
    state,
    flow,
    mag,
    out,
    swap,
    turn,
    leg_fwd,
    leg_back,
    coeffs,
    table,
    table_back,
    lhs,
    fields,
    prods,
    xs,
    xr,
    ys,
    yr,
    zs,
    zr,
    zbs,
    zbr,
    ybs,
    ybr,
    xbr,
    send_sems,
    recv_sems,
    own_sems,
    load_sems,
    store_sems,
):
    my = lax.axis_index("rad")
    ang = lax.axis_index("ang")
    mx = ang // NZ
    mz = ang % NZ
    upper = mx // 2
    device = my * (NX * NZ) + ang

    loads = [
        pltpu.make_async_copy(state_ref.at[2 * g : 2 * g + 2], state.at[2 * g : 2 * g + 2], load_sems.at[g])
        for g in range(NG)
    ]
    loads += [
        pltpu.make_async_copy(flow_ref, flow, load_sems.at[NG]),
        pltpu.make_async_copy(mag_ref, mag, load_sems.at[NG + 1]),
    ]
    stores = [
        pltpu.make_async_copy(out.at[2 * g : 2 * g + 2], out_ref.at[2 * g : 2 * g + 2], store_sems.at[g])
        for g in range(NG)
    ]
    for load in loads:
        load.start()

    def at_x(x):
        return (my, x * NZ + mz)

    def at_y(y):
        return (y, ang)

    def at_z(z):
        return (my, mx * NZ + z)

    barrier = pltpu.get_barrier_semaphore()

    @pl.loop(1, NX)
    def _(d):
        pl.semaphore_signal(barrier, inc=1, device_id=at_x((mx + d) % NX), device_id_type=MESH)

    @pl.loop(1, NY)
    def _(d):
        pl.semaphore_signal(barrier, inc=1, device_id=at_y((my + d) % NY), device_id_type=MESH)

    @pl.loop(1, NZ)
    def _(d):
        pl.semaphore_signal(barrier, inc=1, device_id=at_z((mz + d) % NZ), device_id_type=MESH)

    rings = (
        (NX, mx, at_x, lambda q, x: xs.at[q, x], lambda q: xr.at[q, mx], xr),
        (NY, my, at_y, lambda q, y: ys.at[q, y], lambda q: yr.at[q, my], yr),
        (NZ, mz, at_z, lambda q, z: zs.at[q, z], lambda q: zr.at[q, mz], zr),
        (NZ, mz, at_z, lambda q, z: zbs.at[q, z], lambda q: zbr.at[q, mz], zbr),
        (NY, my, at_y, lambda q, y: ybs.at[q, y], lambda q: ybr.at[q, my], ybr),
        (NX, mx, at_x, lambda q, x: ybr.at[q, :, x % 2], lambda q: xbr.at[q, mx], xbr),
    )

    def own(k, q):
        _, me, _, source, target, _ = rings[k]
        return pltpu.make_async_copy(source(q, me), target(q), own_sems.at[k, q])

    def send(k, q):
        size, me, where, source, target, _ = rings[k]
        own(k, q).start()

        @pl.loop(1, size)
        def _(d):
            place = (me + d) % size
            pltpu.make_async_remote_copy(
                src_ref=source(q, place),
                dst_ref=target(q),
                send_sem=send_sems.at[k],
                recv_sem=recv_sems.at[k, q],
                device_id=where(place),
                device_id_type=MESH,
            ).start()

    def others(k, q):
        size, me, where, _, _, landing = rings[k]
        region = landing.at[q, pl.ds(0, size - 1)]
        return pltpu.make_async_remote_copy(
            src_ref=region,
            dst_ref=region,
            send_sem=send_sems.at[k],
            recv_sem=recv_sems.at[k, q],
            device_id=where((me + 1) % size),
            device_id_type=MESH,
        )

    def receive(k, q):
        others(k, q).wait_recv()
        own(k, q).wait()

    def all_sent(k):
        size, me, where, _, _, landing = rings[k]
        region = landing.at[:, pl.ds(0, size - 1)]
        pltpu.make_async_remote_copy(
            src_ref=region,
            dst_ref=region,
            send_sem=send_sems.at[k],
            recv_sem=recv_sems.at[k, 0],
            device_id=where((me + 1) % size),
            device_id_type=MESH,
        ).wait_send()

    def slot(pos):
        return (1 - upper) * pos + upper * (1 - pos)

    def live_order(pos):
        s = slot(pos)
        live = s < counts_ref[device]
        order = jnp.where(live, assign_ref[s, device], 0)
        return order, jnp.where(live, 511 - order, -1)

    @pl.loop(0, 4)
    def _(b):
        row = iota((256, 1024), 0) + b * 256
        col = iota((256, 1024), 1)
        image = (row % 128) // 16 * 128 + row // 128 * 16 + row % 16
        swap[pl.ds(pl.multiple_of(b * 256, 256), 256), :] = jnp.where(col == image, 1.0, 0.0).astype(BF16)

    def legendre_rows(pos, i):
        _, top = live_order(pos)
        rows = leg_ref[slot(pos)]
        rows = jnp.where(iota((192, 256), 1) <= top, rows.astype(F32), 0.0).astype(BF16)
        r = iota((128, 192), 0)
        pick = jnp.where(iota((128, 192), 1) == 3 * (r // 32 * 16 + r % 16) + i, 1.0, 0.0).astype(BF16)
        picked = dot(pick, rows)
        odd_n = iota((128, 256), 1) % 2
        south = iota((128, 256), 0) // 16 % 2
        return picked, odd_n, south

    for i in range(NC):
        for pos in range(2):
            picked, odd_n, south = legendre_rows(pos, i)
            leg_fwd[i, pos * 128 : (pos + 1) * 128, :] = jnp.where(odd_n * south == 1, -picked, picked).astype(BF16)

    def shuffle(g):
        loads[g].wait()
        joined = jnp.concatenate(
            [state[2 * g + cc, x, slot(pos)] for pos in range(2) for x in range(2) for cc in range(2)], axis=1
        )
        for b in range(4):
            coeffs[g, :, b * 256 : (b + 1) * 256] = dot(joined, swap[:, b * 256 : (b + 1) * 256]).astype(BF16)

    def synthesis(q):
        first = iota((128, 256), 1) % 128 < 64
        for b in range(4):
            both = dot(leg_fwd[q // NG], coeffs[q % NG, :, b * 256 : (b + 1) * 256])
            grid = jnp.where(first, both[:128], both[128:]).astype(BF16)
            xs[q, :, :, b * 256 : (b + 1) * 256] = grid.reshape(NX, 32, 256)
        send(0, q)

    shuffle(0)
    pl.semaphore_wait(barrier, NX + NY + NZ - 3)
    synthesis(0)
    shuffle(1)
    synthesis(1)
    shuffle(2)
    synthesis(2)

    a = iota((512, 512), 0)
    b = iota((512, 512), 1)
    image = (a % 16) * 32 + a // 16 % 2 * 16 + a // 32
    turn[...] = jnp.where(b == image, 1.0, 0.0).astype(BF16)

    def transposed_legendre():
        for i in range(NC):
            for pos in range(2):
                picked, odd_n, south = legendre_rows(pos, i)
                kept = jnp.where(odd_n == south, picked, 0.0)
                leg_back[pos, :, i * 128 : (i + 1) * 128] = kept.T.astype(BF16)

    def tables():
        held = assign_rows_ref[...]
        held = jnp.where(iota((2, 512), 0) < counts_row_ref[...], held, 0)
        digits = jnp.concatenate([held >> 1, held & 1], axis=0).astype(F32).astype(BF16)
        place = iota((256, 512), 0)
        place = place // 2 % 8 * 64 + place % 2 * 16 + place // 16
        lane = iota((256, 512), 1)
        low = dot(jnp.where(lane == place, 1.0, 0.0).astype(BF16), digits, ((1,), (1,)))
        high = dot(jnp.where(lane == place + 32, 1.0, 0.0).astype(BF16), digits, ((1,), (1,)))
        scale = 1.0 / math.sqrt(512)
        for pos in range(2):
            m = 2.0 * (low[:, pos : pos + 1] + high[:, 1 - pos : 2 - pos]) + (
                low[:, 2 + pos : 3 + pos] + high[:, 3 - pos : 4 - pos]
            )
            m = m.astype(jnp.int32)
            lane = iota((256, 128), 1)
            fine = (m * lane & 1023).astype(F32) * (2.0 * math.pi / 1024)
            cos_fine = jnp.cos(fine) * scale
            sin_fine = jnp.sin(fine) * scale
            coarse = (m * lane & 7).astype(F32) * (2.0 * math.pi / 8)
            cos_coarse = jnp.cos(coarse)
            sin_coarse = jnp.sin(coarse)
            back = jnp.where(m == 0, 0.5, 1.0)
            for k in range(8):
                ck = cos_coarse[:, k : k + 1]
                sk = sin_coarse[:, k : k + 1]
                re = (cos_fine * ck - sin_fine * sk).astype(BF16)
                im = (-(sin_fine * ck + cos_fine * sk)).astype(BF16)
                lanes = slice(k * 128, (k + 1) * 128)
                table[pos * 512 : pos * 512 + 256, lanes] = re
                table[pos * 512 + 256 : pos * 512 + 512, lanes] = im
                table_back[pos * 512 : pos * 512 + 256, lanes] = (re.astype(F32) * back).astype(BF16)
                table_back[pos * 512 + 256 : pos * 512 + 512, lanes] = (im.astype(F32) * back).astype(BF16)

    def fold(q):
        receive(0, q)
        for p in range(2):
            pair = xr[q, p] + xr[q, p + 2]
            for y in range(NY):
                ys[q, y, p] = pair[:, y * 128 : (y + 1) * 128]
        send(1, q)

    def spread(q):
        receive(1, q)
        zs[q] = dot(turn[...], yr[q].reshape(512, 128)).astype(BF16).reshape(NZ, 32, 128)
        send(2, q)

    def physics(i):
        for g in range(NG):
            receive(2, NG * i + g)
            for h in range(2):
                block = zr[NG * i + g, :, h * 16 : (h + 1) * 16, :].reshape(256, 128).T
                for p in range(4):
                    row = h * 96 + g * 32
                    lhs[row : row + 32, p * 256 : (p + 1) * 256] = block[p * 32 : (p + 1) * 32]

        @pl.loop(0, 4)
        def _(b):
            lanes = pl.ds(pl.multiple_of(b * 256, 256), 256)
            fields[:, lanes] = dot(lhs[...], table[:, lanes])

        row_t = (iota((8, 128), 0) * 0 + ang * NC + i).astype(F32)
        north = (row_t + 0.5) * (math.pi / 384)
        for h in range(2):
            colat = math.pi - north if h == 1 else north
            along = (coriolis * jnp.cos(colat))[0:1, 0:1]
            across = (-coriolis * jnp.sin(colat))[0:1, 0:1]
            weight = (math.pi / 2 * jnp.sin(colat))[0:1, 0:1]

            @pl.loop(0, 4)
            def _(b):
                lanes = pl.ds(pl.multiple_of(b * 256, 256), 256)
                u = [fields[h * 96 + c * 16 : h * 96 + (c + 1) * 16, lanes] for c in range(3)]
                v = [fields[h * 96 + (c + 3) * 16 : h * 96 + (c + 4) * 16, lanes] for c in range(3)]
                w = [flow[c, 2 * i + h, :, lanes].astype(F32) for c in range(3)]
                f = [mag[c, 2 * i + h, :, lanes].astype(F32) for c in range(3)]
                spin = [w[0] + along, w[1] + across, w[2]]
                for c in range(3):
                    n, o = (c + 1) % 3, (c + 2) % 3
                    momentum = (u[n] * spin[o] - u[o] * spin[n]) + (f[n] * v[o] - f[o] * v[n])
                    induction = (u[n] * f[o] - u[o] * f[n]) + (w[n] * v[o] - w[o] * v[n])
                    row = h * 96 + c * 16
                    prods[row : row + 16, lanes] = (momentum * weight).astype(BF16)
                    prods[row + 48 : row + 64, lanes] = (induction * weight).astype(BF16)

        @pl.loop(0, 4)
        def _(p):
            rows = pl.ds(pl.multiple_of(p * 256, 256), 256)
            returned = dot(prods[...], table_back[rows, :], ((1,), (1,)))
            returned = returned.astype(BF16).astype(F32)
            n, s = returned[:96], returned[96:]
            fields[0:96, rows] = n + s
            fields[96:192, rows] = n - s

        for g in range(NG):
            for h in range(2):
                row = h * 96 + g * 32
                block = jnp.concatenate([fields[row : row + 32, p * 256 : (p + 1) * 256] for p in range(4)], axis=0)
                zbs[NG * i + g, :, h * 16 : (h + 1) * 16, :] = block.T.astype(BF16).reshape(NZ, 16, 128)
            send(3, NG * i + g)

    def gather(q):
        receive(3, q)
        ybs[q] = dot(turn[...], zbr[q].reshape(512, 128)).astype(BF16).reshape(NY, 2, 32, 128)
        send(4, q)

    def unfold(q):
        receive(4, q)
        send(5, q)

    def finish(g):
        for i in range(NC):
            receive(5, NG * i + g)
        parts = []
        for b in range(4):
            rows = jnp.concatenate(
                [
                    jnp.concatenate([xbr[NG * i + g, :, 2 * b + e].reshape(128, 128) for i in range(NC)], axis=0)
                    for e in range(2)
                ],
                axis=1,
            )
            first = iota((256, 256), 1) % 128 < 64
            parts.append(jnp.where(first, dot(leg_back[0], rows), dot(leg_back[1], rows)).astype(BF16))
        nonlinear = jnp.concatenate(parts, axis=1)
        for pos in range(2):
            order, top = live_order(pos)
            n = iota((256, 128), 0)
            degree = (order + n).astype(F32)
            damping = jnp.where(n <= top, 1.0 / (1.0 + degree * (degree + 1.0) / 65536.0), 0.0)
            for x in range(2):
                j = pos * 4 + x * 2
                terms = dot(nonlinear, swap[:, j * 128 : (j + 2) * 128]).astype(BF16)
                for cc in range(2):
                    c = 2 * g + cc
                    joined = jnp.concatenate([state[c, x, slot(pos)], terms[:, cc * 128 : (cc + 1) * 128]], axis=1)
                    stepped = dot(joined, ops_ref[c // 3], ((1,), (1,)))
                    out[c, x, slot(pos)] = (stepped * damping).astype(BF16)
        stores[g].start()

    @pl.loop(0, 17)
    def _(step):
        @pl.when(step < 6)
        def _():
            synthesis(step + 3)

        @pl.when(step < NQ)
        def _():
            fold(step)

        @pl.when(jnp.logical_and(step >= 1, step < NQ + 1))
        def _():
            spread(step - 1)

        @pl.when(step == 1)
        def _():
            tables()

        @pl.when(step == 2)
        def _():
            transposed_legendre()
            loads[NG].wait()
            loads[NG + 1].wait()

        for i in range(NC):

            @pl.when(step == 3 * i + 4)
            def _():
                physics(i)

        @pl.when(jnp.logical_and(step >= 7, step < NQ + 7))
        def _():
            gather(step - 7)

        @pl.when(step >= 8)
        def _():
            unfold(step - 8)

        @pl.when(step == 15)
        def _():
            finish(0)

    finish(1)
    finish(2)
    for k in range(6):
        all_sent(k)
    for store in stores:
        store.wait()


def per_device(state, legendre, radial_ops, base_flow, base_field, assign, counts):
    vmem = pl.BlockSpec(memory_space=pltpu.VMEM)
    smem = pl.BlockSpec(memory_space=pltpu.SMEM)
    hbm = pl.BlockSpec(memory_space=pl.ANY)
    dma = pltpu.SemaphoreType.DMA
    assign_rows = assign.T
    return pl.pallas_call(
        kernel,
        out_shape=jax.ShapeDtypeStruct(state.shape, BF16),
        in_specs=[smem, smem, vmem, vmem, vmem, vmem, hbm, hbm, hbm],
        out_specs=hbm,
        scratch_shapes=[
            pltpu.VMEM(state.shape, BF16),
            pltpu.VMEM(base_flow.shape, BF16),
            pltpu.VMEM(base_field.shape, BF16),
            pltpu.VMEM(state.shape, BF16),
            pltpu.VMEM((1024, 1024), BF16),
            pltpu.VMEM((512, 512), BF16),
            pltpu.VMEM((NC, 256, 256), BF16),
            pltpu.VMEM((2, 256, 384), BF16),
            pltpu.VMEM((NG, 256, 1024), BF16),
            pltpu.VMEM((1024, 1024), BF16),
            pltpu.VMEM((1024, 1024), BF16),
            pltpu.VMEM((192, 1024), BF16),
            pltpu.VMEM((192, 1024), F32),
            pltpu.VMEM((192, 1024), BF16),
            pltpu.VMEM((NQ, NX, 32, 1024), BF16),
            pltpu.VMEM((NQ, NX, 32, 1024), BF16),
            pltpu.VMEM((NQ, NY, 2, 32, 128), BF16),
            pltpu.VMEM((NQ, NY, 2, 32, 128), BF16),
            pltpu.VMEM((NQ, NZ, 32, 128), BF16),
            pltpu.VMEM((NQ, NZ, 32, 128), BF16),
            pltpu.VMEM((NQ, NZ, 32, 128), BF16),
            pltpu.VMEM((NQ, NZ, 32, 128), BF16),
            pltpu.VMEM((NQ, NY, 2, 32, 128), BF16),
            pltpu.VMEM((NQ, NY, 2, 32, 128), BF16),
            pltpu.VMEM((NQ, NX, NY, 32, 128), BF16),
            dma((6,)),
            dma((6, NQ)),
            dma((6, NQ)),
            dma((NG + 2,)),
            dma((NG,)),
        ],
        compiler_params=pltpu.CompilerParams(
            collective_id=0, has_side_effects=True, vmem_limit_bytes=56 * 1024 * 1024
        ),
    )(
        assign_rows,
        counts,
        assign_rows,
        counts.reshape(1, -1),
        legendre,
        radial_ops,
        state,
        base_flow,
        base_field,
    )


def solution(mesh):
    placed = (
        P(None, None, ("rad", "ang"), None, None),
        P(("rad", "ang"), None, None),
        P(),
        P(None, "ang", "rad", None),
        P(None, "ang", "rad", None),
        P(),
        P(),
    )
    return jax.shard_map(
        per_device,
        mesh=mesh,
        in_specs=placed,
        out_specs=P(None, None, ("rad", "ang"), None, None),
        check_vma=False,
    )
```

```python
import math

import jax
import jax.numpy as jnp
from jax import lax
from jax.experimental import pallas as pl
from jax.experimental.pallas import tpu as pltpu
from jax.sharding import PartitionSpec as P

F32 = jnp.float32
BF16 = jnp.bfloat16
MESH = pl.DeviceIdType.MESH

NX = 4
NZ = 16
NY = 8
NC = 3
NG = 3
NQ = NC * NG
AHEAD = 3
SPREAD_LAG = 2
PHYSICS_LAG = 7
GATHER_LAG = 10
UNFOLD_LAG = 12
coriolis = 3.0


def iota(shape, axis):
    return lax.broadcasted_iota(jnp.int32, shape, axis)


def dot(a, b, dims=((1,), (0,))):
    return lax.dot_general(a, b, (dims, ((), ())), preferred_element_type=F32)


def kernel(
    assign_ref,
    counts_ref,
    assign_rows_ref,
    counts_row_ref,
    leg_ref,
    ops_ref,
    state_ref,
    flow_ref,
    mag_ref,
    out_ref,
    state,
    flow,
    mag,
    out,
    swap,
    turn,
    leg_fwd,
    leg_back,
    coeffs,
    table,
    table_back,
    lhs,
    fields,
    prods,
    xs,
    xr,
    ys,
    yr,
    zs,
    zr,
    zbs,
    zbr,
    ybs,
    ybr,
    xbr,
    send_sems,
    recv_sems,
    own_sems,
    load_sems,
    store_sems,
):
    my = lax.axis_index("rad")
    ang = lax.axis_index("ang")
    mx = ang // NZ
    mz = ang % NZ
    upper = mx // 2
    device = my * (NX * NZ) + ang

    loads = [
        pltpu.make_async_copy(state_ref.at[2 * g : 2 * g + 2], state.at[2 * g : 2 * g + 2], load_sems.at[g])
        for g in range(NG)
    ]
    loads += [
        pltpu.make_async_copy(flow_ref, flow, load_sems.at[NG]),
        pltpu.make_async_copy(mag_ref, mag, load_sems.at[NG + 1]),
    ]
    stores = [
        pltpu.make_async_copy(out.at[2 * g : 2 * g + 2], out_ref.at[2 * g : 2 * g + 2], store_sems.at[g])
        for g in range(NG)
    ]
    for load in loads:
        load.start()

    def at_x(x):
        return (my, x * NZ + mz)

    def at_y(y):
        return (y, ang)

    def at_z(z):
        return (my, mx * NZ + z)

    barrier = pltpu.get_barrier_semaphore()

    @pl.loop(1, NX)
    def _(d):
        pl.semaphore_signal(barrier, inc=1, device_id=at_x((mx + d) % NX), device_id_type=MESH)

    @pl.loop(1, NY)
    def _(d):
        pl.semaphore_signal(barrier, inc=1, device_id=at_y((my + d) % NY), device_id_type=MESH)

    @pl.loop(1, NZ)
    def _(d):
        pl.semaphore_signal(barrier, inc=1, device_id=at_z((mz + d) % NZ), device_id_type=MESH)

    rings = (
        (NX, mx, at_x, lambda q, x: xs.at[q, x], lambda q: xr.at[q, mx], xr),
        (NY, my, at_y, lambda q, y: ys.at[q, y], lambda q: yr.at[q, my], yr),
        (NZ, mz, at_z, lambda q, z: zs.at[q, z], lambda q: zr.at[q, mz], zr),
        (NZ, mz, at_z, lambda q, z: zbs.at[q, z], lambda q: zbr.at[q, mz], zbr),
        (NY, my, at_y, lambda q, y: ybs.at[q, y], lambda q: ybr.at[q, my], ybr),
        (NX, mx, at_x, lambda q, x: ybr.at[q, :, x % 2], lambda q: xbr.at[q, mx], xbr),
    )

    def own(k, q):
        _, me, _, source, target, _ = rings[k]
        return pltpu.make_async_copy(source(q, me), target(q), own_sems.at[k, q])

    def send(k, q):
        size, me, where, source, target, _ = rings[k]
        own(k, q).start()

        @pl.loop(1, size)
        def _(d):
            place = (me + d) % size
            pltpu.make_async_remote_copy(
                src_ref=source(q, place),
                dst_ref=target(q),
                send_sem=send_sems.at[k],
                recv_sem=recv_sems.at[k, q],
                device_id=where(place),
                device_id_type=MESH,
            ).start()

    def others(k, q):
        size, me, where, _, _, landing = rings[k]
        region = landing.at[q, pl.ds(0, size - 1)]
        return pltpu.make_async_remote_copy(
            src_ref=region,
            dst_ref=region,
            send_sem=send_sems.at[k],
            recv_sem=recv_sems.at[k, q],
            device_id=where((me + 1) % size),
            device_id_type=MESH,
        )

    def receive(k, q):
        others(k, q).wait_recv()
        own(k, q).wait()

    def all_sent(k):
        size, me, where, _, _, landing = rings[k]
        region = landing.at[:, pl.ds(0, size - 1)]
        pltpu.make_async_remote_copy(
            src_ref=region,
            dst_ref=region,
            send_sem=send_sems.at[k],
            recv_sem=recv_sems.at[k, 0],
            device_id=where((me + 1) % size),
            device_id_type=MESH,
        ).wait_send()

    def slot(pos):
        return (1 - upper) * pos + upper * (1 - pos)

    def live_order(pos):
        s = slot(pos)
        live = s < counts_ref[device]
        order = jnp.where(live, assign_ref[s, device], 0)
        return order, jnp.where(live, 511 - order, -1)

    @pl.loop(0, 4)
    def _(b):
        row = iota((256, 1024), 0) + b * 256
        col = iota((256, 1024), 1)
        image = (row % 128) // 16 * 128 + row // 128 * 16 + row % 16
        swap[pl.ds(pl.multiple_of(b * 256, 256), 256), :] = jnp.where(col == image, 1.0, 0.0).astype(BF16)

    def legendre_rows(pos, i):
        _, top = live_order(pos)
        rows = leg_ref[slot(pos)]
        rows = jnp.where(iota((192, 256), 1) <= top, rows.astype(F32), 0.0).astype(BF16)
        r = iota((128, 192), 0)
        pick = jnp.where(iota((128, 192), 1) == 3 * (r // 32 * 16 + r % 16) + i, 1.0, 0.0).astype(BF16)
        picked = dot(pick, rows)
        odd_n = iota((128, 256), 1) % 2
        south = iota((128, 256), 0) // 16 % 2
        return picked, odd_n, south

    def forward_legendre(i):
        for pos in range(2):
            picked, odd_n, south = legendre_rows(pos, i)
            leg_fwd[i, pos * 128 : (pos + 1) * 128, :] = jnp.where(odd_n * south == 1, -picked, picked).astype(BF16)

    def shuffle(g):
        loads[g].wait()
        joined = jnp.concatenate(
            [state[2 * g + cc, x, slot(pos)] for pos in range(2) for x in range(2) for cc in range(2)], axis=1
        )
        for b in range(4):
            coeffs[g, :, b * 256 : (b + 1) * 256] = dot(joined, swap[:, b * 256 : (b + 1) * 256]).astype(BF16)

    def synthesis(q):
        first = iota((128, 256), 1) % 128 < 64
        for b in range(4):
            both = dot(leg_fwd[q // NG], coeffs[q % NG, :, b * 256 : (b + 1) * 256])
            grid = jnp.where(first, both[:128], both[128:]).astype(BF16)
            xs[q, :, :, b * 256 : (b + 1) * 256] = grid.reshape(NX, 32, 256)
        send(0, q)

    forward_legendre(0)
    shuffle(0)
    pl.semaphore_wait(barrier, NX + NY + NZ - 3)
    synthesis(0)
    shuffle(1)
    synthesis(1)
    shuffle(2)
    synthesis(2)
    forward_legendre(1)
    forward_legendre(2)

    a = iota((512, 512), 0)
    b = iota((512, 512), 1)
    image = (a % 16) * 32 + a // 16 % 2 * 16 + a // 32
    turn[...] = jnp.where(b == image, 1.0, 0.0).astype(BF16)

    def transposed_legendre():
        for i in range(NC):
            for pos in range(2):
                picked, odd_n, south = legendre_rows(pos, i)
                kept = jnp.where(odd_n == south, picked, 0.0)
                leg_back[pos, :, i * 128 : (i + 1) * 128] = kept.T.astype(BF16)

    def tables():
        held = assign_rows_ref[...]
        held = jnp.where(iota((2, 512), 0) < counts_row_ref[...], held, 0)
        digits = jnp.concatenate([held >> 1, held & 1], axis=0).astype(F32).astype(BF16)
        place = iota((256, 512), 0)
        place = place // 2 % 8 * 64 + place % 2 * 16 + place // 16
        lane = iota((256, 512), 1)
        low = dot(jnp.where(lane == place, 1.0, 0.0).astype(BF16), digits, ((1,), (1,)))
        high = dot(jnp.where(lane == place + 32, 1.0, 0.0).astype(BF16), digits, ((1,), (1,)))
        scale = 1.0 / math.sqrt(512)
        for pos in range(2):
            m = 2.0 * (low[:, pos : pos + 1] + high[:, 1 - pos : 2 - pos]) + (
                low[:, 2 + pos : 3 + pos] + high[:, 3 - pos : 4 - pos]
            )
            m = m.astype(jnp.int32)
            lane = iota((256, 128), 1)
            fine = (m * lane & 1023).astype(F32) * (2.0 * math.pi / 1024)
            cos_fine = jnp.cos(fine) * scale
            sin_fine = jnp.sin(fine) * scale
            coarse = (m * lane & 7).astype(F32) * (2.0 * math.pi / 8)
            cos_coarse = jnp.cos(coarse)
            sin_coarse = jnp.sin(coarse)
            back = jnp.where(m == 0, 0.5, 1.0)
            for k in range(8):
                ck = cos_coarse[:, k : k + 1]
                sk = sin_coarse[:, k : k + 1]
                re = (cos_fine * ck - sin_fine * sk).astype(BF16)
                im = (-(sin_fine * ck + cos_fine * sk)).astype(BF16)
                lanes = slice(k * 128, (k + 1) * 128)
                table[pos * 512 : pos * 512 + 256, lanes] = re
                table[pos * 512 + 256 : pos * 512 + 512, lanes] = im
                table_back[pos * 512 : pos * 512 + 256, lanes] = (re.astype(F32) * back).astype(BF16)
                table_back[pos * 512 + 256 : pos * 512 + 512, lanes] = (im.astype(F32) * back).astype(BF16)

    def fold(q):
        receive(0, q)
        for p in range(2):
            pair = xr[q, p] + xr[q, p + 2]
            for y in range(NY):
                ys[q, y, p] = pair[:, y * 128 : (y + 1) * 128]
        send(1, q)

    def spread(q):
        receive(1, q)
        zs[q] = dot(turn[...], yr[q].reshape(512, 128)).astype(BF16).reshape(NZ, 32, 128)
        send(2, q)

    def physics(i):
        for g in range(NG):
            receive(2, NG * i + g)
            for h in range(2):
                block = zr[NG * i + g, :, h * 16 : (h + 1) * 16, :].reshape(256, 128).T
                for p in range(4):
                    row = h * 96 + g * 32
                    lhs[row : row + 32, p * 256 : (p + 1) * 256] = block[p * 32 : (p + 1) * 32]

        @pl.loop(0, 4)
        def _(b):
            lanes = pl.ds(pl.multiple_of(b * 256, 256), 256)
            fields[:, lanes] = dot(lhs[...], table[:, lanes])

        row_t = (iota((8, 128), 0) * 0 + ang * NC + i).astype(F32)
        north = (row_t + 0.5) * (math.pi / 384)
        for h in range(2):
            colat = math.pi - north if h == 1 else north
            along = (coriolis * jnp.cos(colat))[0:1, 0:1]
            across = (-coriolis * jnp.sin(colat))[0:1, 0:1]
            weight = (math.pi / 2 * jnp.sin(colat))[0:1, 0:1]

            @pl.loop(0, 4)
            def _(b):
                lanes = pl.ds(pl.multiple_of(b * 256, 256), 256)
                u = [fields[h * 96 + c * 16 : h * 96 + (c + 1) * 16, lanes] for c in range(3)]
                v = [fields[h * 96 + (c + 3) * 16 : h * 96 + (c + 4) * 16, lanes] for c in range(3)]
                w = [flow[c, 2 * i + h, :, lanes].astype(F32) for c in range(3)]
                f = [mag[c, 2 * i + h, :, lanes].astype(F32) for c in range(3)]
                spin = [w[0] + along, w[1] + across, w[2]]
                for c in range(3):
                    n, o = (c + 1) % 3, (c + 2) % 3
                    momentum = (u[n] * spin[o] - u[o] * spin[n]) + (f[n] * v[o] - f[o] * v[n])
                    induction = (u[n] * f[o] - u[o] * f[n]) + (w[n] * v[o] - w[o] * v[n])
                    row = h * 96 + c * 16
                    prods[row : row + 16, lanes] = (momentum * weight).astype(BF16)
                    prods[row + 48 : row + 64, lanes] = (induction * weight).astype(BF16)

        @pl.loop(0, 4)
        def _(p):
            rows = pl.ds(pl.multiple_of(p * 256, 256), 256)
            returned = dot(prods[...], table_back[rows, :], ((1,), (1,)))
            returned = returned.astype(BF16).astype(F32)
            n, s = returned[:96], returned[96:]
            fields[0:96, rows] = n + s
            fields[96:192, rows] = n - s

        for g in range(NG):
            for h in range(2):
                row = h * 96 + g * 32
                block = jnp.concatenate([fields[row : row + 32, p * 256 : (p + 1) * 256] for p in range(4)], axis=0)
                zbs[NG * i + g, :, h * 16 : (h + 1) * 16, :] = block.T.astype(BF16).reshape(NZ, 16, 128)
            send(3, NG * i + g)

    def gather(q):
        receive(3, q)
        ybs[q] = dot(turn[...], zbr[q].reshape(512, 128)).astype(BF16).reshape(NY, 2, 32, 128)
        send(4, q)

    def unfold(q):
        receive(4, q)
        send(5, q)

    def finish(g):
        for i in range(NC):
            receive(5, NG * i + g)
        parts = []
        for b in range(4):
            rows = jnp.concatenate(
                [
                    jnp.concatenate([xbr[NG * i + g, :, 2 * b + e].reshape(128, 128) for i in range(NC)], axis=0)
                    for e in range(2)
                ],
                axis=1,
            )
            first = iota((256, 256), 1) % 128 < 64
            parts.append(jnp.where(first, dot(leg_back[0], rows), dot(leg_back[1], rows)).astype(BF16))
        nonlinear = jnp.concatenate(parts, axis=1)
        for pos in range(2):
            order, top = live_order(pos)
            n = iota((256, 128), 0)
            degree = (order + n).astype(F32)
            damping = jnp.where(n <= top, 1.0 / (1.0 + degree * (degree + 1.0) / 65536.0), 0.0)
            for x in range(2):
                j = pos * 4 + x * 2
                terms = dot(nonlinear, swap[:, j * 128 : (j + 2) * 128]).astype(BF16)
                for cc in range(2):
                    c = 2 * g + cc
                    joined = jnp.concatenate([state[c, x, slot(pos)], terms[:, cc * 128 : (cc + 1) * 128]], axis=1)
                    stepped = dot(joined, ops_ref[c // 3], ((1,), (1,)))
                    out[c, x, slot(pos)] = (stepped * damping).astype(BF16)
        stores[g].start()

    def at(step, lag, work, every=1):
        q = (step - lag) // every

        @pl.when((step >= lag) & (step < lag + NQ) & ((step - lag) % every == 0))
        def _():
            work(q)

    @pl.loop(0, UNFOLD_LAG + NQ)
    def _(step):
        at(step, -AHEAD, synthesis)
        at(step, 0, fold)
        at(step, SPREAD_LAG, spread)

        @pl.when(step == 1)
        def _():
            tables()

        @pl.when(step == 2)
        def _():
            transposed_legendre()
            loads[NG].wait()
            loads[NG + 1].wait()

        at(step, PHYSICS_LAG, physics, NG)
        at(step, GATHER_LAG, gather)
        at(step, UNFOLD_LAG, unfold)

    finish(0)
    finish(1)
    finish(2)
    for k in range(6):
        all_sent(k)
    for store in stores:
        store.wait()


def per_device(state, legendre, radial_ops, base_flow, base_field, assign, counts):
    vmem = pl.BlockSpec(memory_space=pltpu.VMEM)
    smem = pl.BlockSpec(memory_space=pltpu.SMEM)
    hbm = pl.BlockSpec(memory_space=pl.ANY)
    dma = pltpu.SemaphoreType.DMA
    assign_rows = assign.T
    return pl.pallas_call(
        kernel,
        out_shape=jax.ShapeDtypeStruct(state.shape, BF16),
        in_specs=[smem, smem, vmem, vmem, vmem, vmem, hbm, hbm, hbm],
        out_specs=hbm,
        scratch_shapes=[
            pltpu.VMEM(state.shape, BF16),
            pltpu.VMEM(base_flow.shape, BF16),
            pltpu.VMEM(base_field.shape, BF16),
            pltpu.VMEM(state.shape, BF16),
            pltpu.VMEM((1024, 1024), BF16),
            pltpu.VMEM((512, 512), BF16),
            pltpu.VMEM((NC, 256, 256), BF16),
            pltpu.VMEM((2, 256, 384), BF16),
            pltpu.VMEM((NG, 256, 1024), BF16),
            pltpu.VMEM((1024, 1024), BF16),
            pltpu.VMEM((1024, 1024), BF16),
            pltpu.VMEM((192, 1024), BF16),
            pltpu.VMEM((192, 1024), F32),
            pltpu.VMEM((192, 1024), BF16),
            pltpu.VMEM((NQ, NX, 32, 1024), BF16),
            pltpu.VMEM((NQ, NX, 32, 1024), BF16),
            pltpu.VMEM((NQ, NY, 2, 32, 128), BF16),
            pltpu.VMEM((NQ, NY, 2, 32, 128), BF16),
            pltpu.VMEM((NQ, NZ, 32, 128), BF16),
            pltpu.VMEM((NQ, NZ, 32, 128), BF16),
            pltpu.VMEM((NQ, NZ, 32, 128), BF16),
            pltpu.VMEM((NQ, NZ, 32, 128), BF16),
            pltpu.VMEM((NQ, NY, 2, 32, 128), BF16),
            pltpu.VMEM((NQ, NY, 2, 32, 128), BF16),
            pltpu.VMEM((NQ, NX, NY, 32, 128), BF16),
            dma((6,)),
            dma((6, NQ)),
            dma((6, NQ)),
            dma((NG + 2,)),
            dma((NG,)),
        ],
        compiler_params=pltpu.CompilerParams(
            collective_id=0, has_side_effects=True, vmem_limit_bytes=56 * 1024 * 1024
        ),
    )(
        assign_rows,
        counts,
        assign_rows,
        counts.reshape(1, -1),
        legendre,
        radial_ops,
        state,
        base_flow,
        base_field,
    )


def solution(mesh):
    placed = (
        P(None, None, ("rad", "ang"), None, None),
        P(("rad", "ang"), None, None),
        P(),
        P(None, "ang", "rad", None),
        P(None, "ang", "rad", None),
        P(),
        P(),
    )
    return jax.shard_map(
        per_device,
        mesh=mesh,
        in_specs=placed,
        out_specs=P(None, None, ("rad", "ang"), None, None),
        check_vma=False,
    )
```

```python
import math

import jax
import jax.numpy as jnp
from jax import lax
from jax.experimental import pallas as pl
from jax.experimental.pallas import tpu as pltpu
from jax.sharding import PartitionSpec as P

F32 = jnp.float32
BF16 = jnp.bfloat16
MESH = pl.DeviceIdType.MESH

NX = 4
NZ = 16
NY = 8
NC = 3
NG = 3
NQ = NC * NG
SCHEDULE = (
    ("gather", 12),
    ("late_table", 7),
    ("unfold", 14),
    ("to_grid", 8),
    ("fold", 0),
    ("spread", 2),
    ("products", 8),
    ("early_table", 0),
    ("synthesis", -3),
    ("from_grid", 9),
    ("transposed_legendre", 4),
)
coriolis = 3.0


def iota(shape, axis):
    return lax.broadcasted_iota(jnp.int32, shape, axis)


def dot(a, b, dims=((1,), (0,))):
    return lax.dot_general(a, b, (dims, ((), ())), preferred_element_type=F32)


def kernel(
    assign_ref,
    counts_ref,
    assign_rows_ref,
    counts_row_ref,
    leg_ref,
    ops_ref,
    state_ref,
    flow_ref,
    mag_ref,
    out_ref,
    state,
    flow,
    mag,
    out,
    swap,
    turn,
    leg_fwd,
    leg_back,
    coeffs,
    table,
    table_back,
    lhs,
    fields,
    prods,
    xs,
    xr,
    ys,
    yr,
    zs,
    zr,
    zbs,
    zbr,
    ybs,
    ybr,
    xbr,
    send_sems,
    recv_sems,
    own_sems,
    load_sems,
    store_sems,
):
    my = lax.axis_index("rad")
    ang = lax.axis_index("ang")
    mx = ang // NZ
    mz = ang % NZ
    upper = mx // 2
    device = my * (NX * NZ) + ang

    loads = [
        pltpu.make_async_copy(state_ref.at[2 * g : 2 * g + 2], state.at[2 * g : 2 * g + 2], load_sems.at[g])
        for g in range(NG)
    ]
    loads += [
        pltpu.make_async_copy(flow_ref, flow, load_sems.at[NG]),
        pltpu.make_async_copy(mag_ref, mag, load_sems.at[NG + 1]),
    ]
    stores = [
        pltpu.make_async_copy(out.at[2 * g : 2 * g + 2], out_ref.at[2 * g : 2 * g + 2], store_sems.at[g])
        for g in range(NG)
    ]
    for load in loads[:NG]:
        load.start()

    def at_x(x):
        return (my, x * NZ + mz)

    def at_y(y):
        return (y, ang)

    def at_z(z):
        return (my, mx * NZ + z)

    barrier = pltpu.get_barrier_semaphore()

    @pl.loop(1, NX)
    def _(d):
        pl.semaphore_signal(barrier, inc=1, device_id=at_x((mx + d) % NX), device_id_type=MESH)

    @pl.loop(1, NY)
    def _(d):
        pl.semaphore_signal(barrier, inc=1, device_id=at_y((my + d) % NY), device_id_type=MESH)

    @pl.loop(1, NZ)
    def _(d):
        pl.semaphore_signal(barrier, inc=1, device_id=at_z((mz + d) % NZ), device_id_type=MESH)

    rings = (
        (NX, mx, at_x, lambda q, x: xs.at[q, x], lambda q: xr.at[q, mx], xr),
        (NY, my, at_y, lambda q, y: ys.at[q, y], lambda q: yr.at[q, my], yr),
        (NZ, mz, at_z, lambda q, z: zs.at[q, z], lambda q: zr.at[q, mz], zr),
        (NZ, mz, at_z, lambda q, z: zbs.at[q, z], lambda q: zbr.at[q, mz], zbr),
        (NY, my, at_y, lambda q, y: ybs.at[q, y], lambda q: ybr.at[q, my], ybr),
        (NX, mx, at_x, lambda q, x: ybr.at[q, :, x % 2], lambda q: xbr.at[q, mx], xbr),
    )

    def own(k, q):
        _, me, _, source, target, _ = rings[k]
        return pltpu.make_async_copy(source(q, me), target(q), own_sems.at[k, q])

    def send(k, q):
        size, me, where, source, target, _ = rings[k]
        own(k, q).start()

        @pl.loop(1, size)
        def _(d):
            place = (me + d) % size
            pltpu.make_async_remote_copy(
                src_ref=source(q, place),
                dst_ref=target(q),
                send_sem=send_sems.at[k],
                recv_sem=recv_sems.at[k, q],
                device_id=where(place),
                device_id_type=MESH,
            ).start()

    def others(k, q):
        size, me, where, _, _, landing = rings[k]
        region = landing.at[q, pl.ds(0, size - 1)]
        return pltpu.make_async_remote_copy(
            src_ref=region,
            dst_ref=region,
            send_sem=send_sems.at[k],
            recv_sem=recv_sems.at[k, q],
            device_id=where((me + 1) % size),
            device_id_type=MESH,
        )

    def receive(k, q):
        others(k, q).wait_recv()
        own(k, q).wait()

    def all_sent(k):
        size, me, where, _, _, landing = rings[k]
        region = landing.at[:, pl.ds(0, size - 1)]
        pltpu.make_async_remote_copy(
            src_ref=region,
            dst_ref=region,
            send_sem=send_sems.at[k],
            recv_sem=recv_sems.at[k, 0],
            device_id=where((me + 1) % size),
            device_id_type=MESH,
        ).wait_send()

    def slot(pos):
        return (1 - upper) * pos + upper * (1 - pos)

    def live_order(pos):
        s = slot(pos)
        live = s < counts_ref[device]
        order = jnp.where(live, assign_ref[s, device], 0)
        return order, jnp.where(live, 511 - order, -1)

    @pl.loop(0, 4)
    def _(b):
        row = iota((256, 1024), 0) + b * 256
        col = iota((256, 1024), 1)
        image = (row % 128) // 16 * 128 + row // 128 * 16 + row % 16
        swap[pl.ds(pl.multiple_of(b * 256, 256), 256), :] = jnp.where(col == image, 1.0, 0.0).astype(BF16)

    def legendre_rows(pos, i):
        _, top = live_order(pos)
        rows = leg_ref[slot(pos)]
        rows = jnp.where(iota((192, 256), 1) <= top, rows.astype(F32), 0.0).astype(BF16)
        r = iota((128, 192), 0)
        pick = jnp.where(iota((128, 192), 1) == 3 * (r // 32 * 16 + r % 16) + i, 1.0, 0.0).astype(BF16)
        picked = dot(pick, rows)
        odd_n = iota((128, 256), 1) % 2
        south = iota((128, 256), 0) // 16 % 2
        return picked, odd_n, south

    def forward_legendre(i):
        for pos in range(2):
            picked, odd_n, south = legendre_rows(pos, i)
            leg_fwd[i, pos * 128 : (pos + 1) * 128, :] = jnp.where(odd_n * south == 1, -picked, picked).astype(BF16)

    def shuffle(g):
        loads[g].wait()
        joined = jnp.concatenate(
            [state[2 * g + cc, x, slot(pos)] for pos in range(2) for x in range(2) for cc in range(2)], axis=1
        )
        for b in range(4):
            coeffs[g, :, b * 256 : (b + 1) * 256] = dot(joined, swap[:, b * 256 : (b + 1) * 256]).astype(BF16)

    def synthesis(q):
        first = iota((128, 256), 1) % 128 < 64
        for b in range(4):
            both = dot(leg_fwd[q // NG], coeffs[q % NG, :, b * 256 : (b + 1) * 256])
            grid = jnp.where(first, both[:128], both[128:]).astype(BF16)
            xs[q, :, :, b * 256 : (b + 1) * 256] = grid.reshape(NX, 32, 256)
        send(0, q)

    forward_legendre(0)
    shuffle(0)
    pl.semaphore_wait(barrier, NX + NY + NZ - 3)
    synthesis(0)
    shuffle(1)
    synthesis(1)
    shuffle(2)
    synthesis(2)
    forward_legendre(1)
    forward_legendre(2)
    for load in loads[NG:]:
        load.start()

    a = iota((512, 512), 0)
    b = iota((512, 512), 1)
    image = (a % 16) * 32 + a // 16 % 2 * 16 + a // 32
    turn[...] = jnp.where(b == image, 1.0, 0.0).astype(BF16)

    def transposed_legendre():
        for i in range(NC):
            for pos in range(2):
                picked, odd_n, south = legendre_rows(pos, i)
                kept = jnp.where(odd_n == south, picked, 0.0)
                leg_back[pos, :, i * 128 : (i + 1) * 128] = kept.T.astype(BF16)

    def make_table(pos):
        held = assign_rows_ref[...]
        held = jnp.where(iota((2, 512), 0) < counts_row_ref[...], held, 0)
        digits = jnp.concatenate([held >> 1, held & 1], axis=0).astype(F32).astype(BF16)
        place = iota((256, 1), 0)
        place = place // 2 % 8 * 64 + place % 2 * 16 + place // 16
        lane = iota((256, 512), 1)
        low = dot(jnp.where(lane == place, 1.0, 0.0).astype(BF16), digits, ((1,), (1,)))
        high = dot(jnp.where(lane == place + 32, 1.0, 0.0).astype(BF16), digits, ((1,), (1,)))
        m = 2.0 * (low[:, pos : pos + 1] + high[:, 1 - pos : 2 - pos]) + (
            low[:, 2 + pos : 3 + pos] + high[:, 3 - pos : 4 - pos]
        )
        m = m.astype(jnp.int32)
        fine = (m * iota((256, 128), 1) & 1023).astype(F32) * (2.0 * math.pi / 1024)
        scale = 1.0 / math.sqrt(512)
        cos_at = jnp.cos(fine)
        sin_at = jnp.sin(fine)
        half_cos = cos_at[:, 64:65]
        half_sin = sin_at[:, 64:65]
        cos_step = 1.0 - 2.0 * half_sin * half_sin
        sin_step = 2.0 * half_sin * half_cos
        cos_at = cos_at * scale
        sin_at = sin_at * scale
        back = jnp.where(m == 0, 0.5, 1.0)
        for k in range(8):
            re = cos_at.astype(BF16)
            im = (-sin_at).astype(BF16)
            lanes = slice(k * 128, (k + 1) * 128)
            table[pos * 512 : pos * 512 + 256, lanes] = re
            table[pos * 512 + 256 : pos * 512 + 512, lanes] = im
            table_back[pos * 512 : pos * 512 + 256, lanes] = (re.astype(F32) * back).astype(BF16)
            table_back[pos * 512 + 256 : pos * 512 + 512, lanes] = (im.astype(F32) * back).astype(BF16)
            cos_at, sin_at = cos_at * cos_step - sin_at * sin_step, sin_at * cos_step + cos_at * sin_step

    def fold(q):
        receive(0, q)
        for p in range(2):
            pair = xr[q, p] + xr[q, p + 2]
            for y in range(NY):
                ys[q, y, p] = pair[:, y * 128 : (y + 1) * 128]
        send(1, q)

    def spread(q):
        receive(1, q)
        zs[q] = dot(turn[...], yr[q].reshape(512, 128)).astype(BF16).reshape(NZ, 32, 128)
        send(2, q)

    def to_grid(i):
        for g in range(NG):
            receive(2, NG * i + g)
            for h in range(2):
                block = zr[NG * i + g, :, h * 16 : (h + 1) * 16, :].reshape(256, 128).T
                for p in range(4):
                    row = h * 96 + g * 32
                    lhs[row : row + 32, p * 256 : (p + 1) * 256] = block[p * 32 : (p + 1) * 32]

        @pl.loop(0, 4)
        def _(b):
            lanes = pl.ds(pl.multiple_of(b * 256, 256), 256)
            fields[:, lanes] = dot(lhs[...], table[:, lanes])

    def products(i):
        row_t = (iota((8, 128), 0) * 0 + ang * NC + i).astype(F32)
        north = (row_t + 0.5) * (math.pi / 384)
        for h in range(2):
            colat = math.pi - north if h == 1 else north
            along = (coriolis * jnp.cos(colat))[0:1, 0:1]
            across = (-coriolis * jnp.sin(colat))[0:1, 0:1]
            weight = (math.pi / 2 * jnp.sin(colat))[0:1, 0:1]

            @pl.loop(0, 4)
            def _(b):
                lanes = pl.ds(pl.multiple_of(b * 256, 256), 256)
                u = [fields[h * 96 + c * 16 : h * 96 + (c + 1) * 16, lanes] for c in range(3)]
                v = [fields[h * 96 + (c + 3) * 16 : h * 96 + (c + 4) * 16, lanes] for c in range(3)]
                w = [flow[c, 2 * i + h, :, lanes].astype(F32) for c in range(3)]
                f = [mag[c, 2 * i + h, :, lanes].astype(F32) for c in range(3)]
                spin = [w[0] + along, w[1] + across, w[2]]
                for c in range(3):
                    n, o = (c + 1) % 3, (c + 2) % 3
                    momentum = (u[n] * spin[o] - u[o] * spin[n]) + (f[n] * v[o] - f[o] * v[n])
                    induction = (u[n] * f[o] - u[o] * f[n]) + (w[n] * v[o] - w[o] * v[n])
                    row = h * 96 + c * 16
                    prods[row : row + 16, lanes] = (momentum * weight).astype(BF16)
                    prods[row + 48 : row + 64, lanes] = (induction * weight).astype(BF16)

    def from_grid(i):
        @pl.loop(0, 4)
        def _(p):
            rows = pl.ds(pl.multiple_of(p * 256, 256), 256)
            returned = dot(prods[...], table_back[rows, :], ((1,), (1,)))
            returned = returned.astype(BF16).astype(F32)
            n, s = returned[:96], returned[96:]
            fields[0:96, rows] = n + s
            fields[96:192, rows] = n - s

        for g in range(NG):
            for h in range(2):
                row = h * 96 + g * 32
                block = jnp.concatenate([fields[row : row + 32, p * 256 : (p + 1) * 256] for p in range(4)], axis=0)
                zbs[NG * i + g, :, h * 16 : (h + 1) * 16, :] = block.T.astype(BF16).reshape(NZ, 16, 128)
            send(3, NG * i + g)

    def gather(q):
        receive(3, q)
        ybs[q] = dot(turn[...], zbr[q].reshape(512, 128)).astype(BF16).reshape(NY, 2, 32, 128)
        send(4, q)

    def unfold(q):
        receive(4, q)
        send(5, q)

    def finish(g):
        for i in range(NC):
            receive(5, NG * i + g)
        parts = []
        for b in range(4):
            rows = jnp.concatenate(
                [
                    jnp.concatenate([xbr[NG * i + g, :, 2 * b + e].reshape(128, 128) for i in range(NC)], axis=0)
                    for e in range(2)
                ],
                axis=1,
            )
            first = iota((256, 256), 1) % 128 < 64
            parts.append(jnp.where(first, dot(leg_back[0], rows), dot(leg_back[1], rows)).astype(BF16))
        nonlinear = jnp.concatenate(parts, axis=1)
        for pos in range(2):
            order, top = live_order(pos)
            n = iota((256, 128), 0)
            degree = (order + n).astype(F32)
            damping = jnp.where(n <= top, 1.0 / (1.0 + degree * (degree + 1.0) / 65536.0), 0.0)
            for x in range(2):
                j = pos * 4 + x * 2
                terms = dot(nonlinear, swap[:, j * 128 : (j + 2) * 128]).astype(BF16)
                for cc in range(2):
                    c = 2 * g + cc
                    joined = jnp.concatenate([state[c, x, slot(pos)], terms[:, cc * 128 : (cc + 1) * 128]], axis=1)
                    stepped = dot(joined, ops_ref[c // 3], ((1,), (1,)))
                    out[c, x, slot(pos)] = (stepped * damping).astype(BF16)
        stores[g].start()

    by_piece = {"synthesis": synthesis, "fold": fold, "spread": spread, "gather": gather, "unfold": unfold}
    by_chunk = {"to_grid": to_grid, "products": products, "from_grid": from_grid}

    def late_table():
        make_table(1)
        loads[NG].wait()
        loads[NG + 1].wait()

    once = {
        "early_table": lambda: make_table(0),
        "late_table": late_table,
        "transposed_legendre": transposed_legendre,
    }

    @pl.loop(0, max(lag for _, lag in SCHEDULE) + NQ)
    def _(step):
        for what, lag in SCHEDULE:
            if what in once:
                due = step == lag
            else:
                due = (step >= lag) & (step < lag + NQ)
            if what in by_chunk:
                due &= (step - lag) % NG == 0

            @pl.when(due)
            def _():
                if what in once:
                    once[what]()
                elif what in by_chunk:
                    by_chunk[what]((step - lag) // NG)
                else:
                    by_piece[what](step - lag)

    finish(0)
    finish(1)
    finish(2)
    for k in range(6):
        all_sent(k)
    for store in stores:
        store.wait()


def per_device(state, legendre, radial_ops, base_flow, base_field, assign, counts):
    vmem = pl.BlockSpec(memory_space=pltpu.VMEM)
    smem = pl.BlockSpec(memory_space=pltpu.SMEM)
    hbm = pl.BlockSpec(memory_space=pl.ANY)
    dma = pltpu.SemaphoreType.DMA
    assign_rows = assign.T
    return pl.pallas_call(
        kernel,
        out_shape=jax.ShapeDtypeStruct(state.shape, BF16),
        in_specs=[smem, smem, vmem, vmem, vmem, vmem, hbm, hbm, hbm],
        out_specs=hbm,
        scratch_shapes=[
            pltpu.VMEM(state.shape, BF16),
            pltpu.VMEM(base_flow.shape, BF16),
            pltpu.VMEM(base_field.shape, BF16),
            pltpu.VMEM(state.shape, BF16),
            pltpu.VMEM((1024, 1024), BF16),
            pltpu.VMEM((512, 512), BF16),
            pltpu.VMEM((NC, 256, 256), BF16),
            pltpu.VMEM((2, 256, 384), BF16),
            pltpu.VMEM((NG, 256, 1024), BF16),
            pltpu.VMEM((1024, 1024), BF16),
            pltpu.VMEM((1024, 1024), BF16),
            pltpu.VMEM((192, 1024), BF16),
            pltpu.VMEM((192, 1024), F32),
            pltpu.VMEM((192, 1024), BF16),
            pltpu.VMEM((NQ, NX, 32, 1024), BF16),
            pltpu.VMEM((NQ, NX, 32, 1024), BF16),
            pltpu.VMEM((NQ, NY, 2, 32, 128), BF16),
            pltpu.VMEM((NQ, NY, 2, 32, 128), BF16),
            pltpu.VMEM((NQ, NZ, 32, 128), BF16),
            pltpu.VMEM((NQ, NZ, 32, 128), BF16),
            pltpu.VMEM((NQ, NZ, 32, 128), BF16),
            pltpu.VMEM((NQ, NZ, 32, 128), BF16),
            pltpu.VMEM((NQ, NY, 2, 32, 128), BF16),
            pltpu.VMEM((NQ, NY, 2, 32, 128), BF16),
            pltpu.VMEM((NQ, NX, NY, 32, 128), BF16),
            dma((6,)),
            dma((6, NQ)),
            dma((6, NQ)),
            dma((NG + 2,)),
            dma((NG,)),
        ],
        compiler_params=pltpu.CompilerParams(
            collective_id=0, has_side_effects=True, vmem_limit_bytes=56 * 1024 * 1024
        ),
    )(
        assign_rows,
        counts,
        assign_rows,
        counts.reshape(1, -1),
        legendre,
        radial_ops,
        state,
        base_flow,
        base_field,
    )


def solution(mesh):
    placed = (
        P(None, None, ("rad", "ang"), None, None),
        P(("rad", "ang"), None, None),
        P(),
        P(None, "ang", "rad", None),
        P(None, "ang", "rad", None),
        P(),
        P(),
    )
    return jax.shard_map(
        per_device,
        mesh=mesh,
        in_specs=placed,
        out_specs=P(None, None, ("rad", "ang"), None, None),
        check_vma=False,
    )
```

```python
import math

import jax
import jax.numpy as jnp
from jax import lax
from jax.experimental import pallas as pl
from jax.experimental.pallas import tpu as pltpu
from jax.sharding import PartitionSpec as P

F32 = jnp.float32
BF16 = jnp.bfloat16
MESH = pl.DeviceIdType.MESH

NX = 4
NZ = 16
NY = 8
NC = 3
NG = 3
NP = NC * NG
NQ = 2 * NP
SCHEDULE = (
    ("to_grid", 0, 8),
    ("early_table", 0, 1),
    ("transposed_legendre", 0, 3),
    ("unfold", 0, 14),
    ("fold", 1, 1),
    ("middle", 1, 3),
    ("products", 0, 8),
    ("unfold", 1, 14),
    ("gather", 1, 11),
    ("late_table", 0, 6),
    ("gather", 0, 11),
    ("synthesis", 0, -3),
    ("from_grid", 0, 9),
    ("middle", 0, 2),
    ("fold", 0, 0),
)
coriolis = 3.0


def iota(shape, axis):
    return lax.broadcasted_iota(jnp.int32, shape, axis)


def dot(a, b, dims=((1,), (0,))):
    return lax.dot_general(a, b, (dims, ((), ())), preferred_element_type=F32)


def kernel(
    assign_ref,
    counts_ref,
    assign_rows_ref,
    counts_row_ref,
    leg_ref,
    ops_ref,
    state_ref,
    flow_ref,
    mag_ref,
    out_ref,
    state,
    flow,
    mag,
    out,
    swap,
    turn,
    leg_fwd,
    leg_back,
    coeffs,
    table,
    table_back,
    lhs,
    fields,
    prods,
    xs,
    xr,
    ys,
    yr,
    zs,
    zr,
    zbs,
    zbr,
    ybs,
    ybr,
    xbr,
    send_sems,
    recv_sems,
    own_sems,
    load_sems,
    store_sems,
):
    my = lax.axis_index("rad")
    ang = lax.axis_index("ang")
    mx = ang // NZ
    mz = ang % NZ
    upper = mx // 2
    device = my * (NX * NZ) + ang

    loads = [
        pltpu.make_async_copy(state_ref.at[2 * g : 2 * g + 2], state.at[2 * g : 2 * g + 2], load_sems.at[g])
        for g in range(NG)
    ]
    loads += [
        pltpu.make_async_copy(flow_ref, flow, load_sems.at[NG]),
        pltpu.make_async_copy(mag_ref, mag, load_sems.at[NG + 1]),
    ]
    stores = [
        pltpu.make_async_copy(out.at[2 * g : 2 * g + 2], out_ref.at[2 * g : 2 * g + 2], store_sems.at[g])
        for g in range(NG)
    ]
    for load in loads[:NG]:
        load.start()

    def at_x(x):
        return (my, x * NZ + mz)

    def at_y(y):
        return (y, ang)

    def at_z(z):
        return (my, mx * NZ + z)

    barrier = pltpu.get_barrier_semaphore()

    @pl.loop(1, NX)
    def _(d):
        pl.semaphore_signal(barrier, inc=1, device_id=at_x((mx + d) % NX), device_id_type=MESH)

    @pl.loop(1, NY)
    def _(d):
        pl.semaphore_signal(barrier, inc=1, device_id=at_y((my + d) % NY), device_id_type=MESH)

    @pl.loop(1, NZ)
    def _(d):
        pl.semaphore_signal(barrier, inc=1, device_id=at_z((mz + d) % NZ), device_id_type=MESH)

    rings = (
        (NX, mx, at_x, lambda q, x: xs.at[q, x], lambda q: xr.at[q, mx], xr),
        (NY, my, at_y, lambda q, y: ys.at[q, y], lambda q: yr.at[q, my], yr),
        (NZ, mz, at_z, lambda q, z: zs.at[q, z], lambda q: zr.at[q, mz], zr),
        (NZ, mz, at_z, lambda q, z: zbs.at[q, z], lambda q: zbr.at[q, mz], zbr),
        (NY, my, at_y, lambda q, y: ybs.at[q, y], lambda q: ybr.at[q, my], ybr),
        (NX, mx, at_x, lambda q, x: ybr.at[q, :, x % 2], lambda q: xbr.at[q, mx], xbr),
    )

    def own(k, q):
        _, me, _, source, target, _ = rings[k]
        return pltpu.make_async_copy(source(q, me), target(q), own_sems.at[k, q])

    def send(k, q):
        size, me, where, source, target, _ = rings[k]
        own(k, q).start()

        @pl.loop(1, size)
        def _(d):
            place = (me + d) % size
            pltpu.make_async_remote_copy(
                src_ref=source(q, place),
                dst_ref=target(q),
                send_sem=send_sems.at[k],
                recv_sem=recv_sems.at[k, q],
                device_id=where(place),
                device_id_type=MESH,
            ).start()

    def others(k, q):
        size, me, where, _, _, landing = rings[k]
        region = landing.at[q, pl.ds(0, size - 1)]
        return pltpu.make_async_remote_copy(
            src_ref=region,
            dst_ref=region,
            send_sem=send_sems.at[k],
            recv_sem=recv_sems.at[k, q],
            device_id=where((me + 1) % size),
            device_id_type=MESH,
        )

    def receive(k, q):
        others(k, q).wait_recv()
        own(k, q).wait()

    def all_sent(k):
        size, me, where, _, _, landing = rings[k]
        region = landing.at[:, pl.ds(0, size - 1)]
        pltpu.make_async_remote_copy(
            src_ref=region,
            dst_ref=region,
            send_sem=send_sems.at[k],
            recv_sem=recv_sems.at[k, 0],
            device_id=where((me + 1) % size),
            device_id_type=MESH,
        ).wait_send()

    def slot(pos):
        return (1 - upper) * pos + upper * (1 - pos)

    def live_order(pos):
        s = slot(pos)
        live = s < counts_ref[device]
        order = jnp.where(live, assign_ref[s, device], 0)
        return order, jnp.where(live, 511 - order, -1)

    @pl.loop(0, 4)
    def _(b):
        row = iota((256, 1024), 0) + b * 256
        col = iota((256, 1024), 1)
        image = (row % 128) // 16 * 128 + row // 128 * 16 + row % 16
        swap[pl.ds(pl.multiple_of(b * 256, 256), 256), :] = jnp.where(col == image, 1.0, 0.0).astype(BF16)

    def legendre_rows(pos, i):
        _, top = live_order(pos)
        rows = leg_ref[slot(pos)]
        rows = jnp.where(iota((192, 256), 1) <= top, rows.astype(F32), 0.0).astype(BF16)
        r = iota((128, 192), 0)
        pick = jnp.where(iota((128, 192), 1) == 3 * (r % 64) + i, 1.0, 0.0).astype(BF16)
        picked = dot(pick, rows)
        odd_n = iota((128, 256), 1) % 2
        south = iota((128, 256), 0) // 64
        return picked, odd_n, south

    def forward_legendre(i):
        for pos in range(2):
            picked, odd_n, south = legendre_rows(pos, i)
            signed = jnp.where(odd_n * south == 1, -picked, picked).astype(BF16)
            for h in range(2):
                row = h * 128 + pos * 64
                leg_fwd[i, row : row + 64, :] = signed[h * 64 : (h + 1) * 64]

    def shuffle(g):
        loads[g].wait()
        joined = jnp.concatenate(
            [state[2 * g + cc, x, slot(pos)] for pos in range(2) for x in range(2) for cc in range(2)], axis=1
        )
        for b in range(4):
            coeffs[g, :, b * 256 : (b + 1) * 256] = dot(joined, swap[:, b * 256 : (b + 1) * 256]).astype(BF16)

    def synthesis(j):
        first = iota((64, 256), 1) % 128 < 64
        for b in range(4):
            both = dot(leg_fwd[j // NG], coeffs[j % NG, :, b * 256 : (b + 1) * 256])
            for h in range(2):
                row = h * 128
                grid = jnp.where(first, both[row : row + 64], both[row + 64 : row + 128]).astype(BF16)
                xs[2 * j + h, :, :, b * 256 : (b + 1) * 256] = grid.reshape(NX, 16, 256)
        send(0, 2 * j)
        send(0, 2 * j + 1)

    forward_legendre(0)
    shuffle(0)
    pl.semaphore_wait(barrier, NX + NY + NZ - 3)
    synthesis(0)
    shuffle(1)
    synthesis(1)
    shuffle(2)
    synthesis(2)
    forward_legendre(1)
    forward_legendre(2)
    for load in loads[NG:]:
        load.start()

    a = iota((256, 256), 0)
    b = iota((256, 256), 1)
    turn[...] = jnp.where(b == a % 16 * 16 + a // 16, 1.0, 0.0).astype(BF16)

    def turned(rows):
        return dot(turn[...], rows.reshape(256, 128)).astype(BF16)

    def by_y(rows):
        return rows.reshape(NY, 2, 16, 128)

    def by_z(rows):
        return rows.reshape(NZ, 16, 128)

    def transposed_legendre():
        for i in range(NC):
            for pos in range(2):
                picked, odd_n, south = legendre_rows(pos, i)
                kept = jnp.where(odd_n == south, picked, 0.0)
                leg_back[pos, :, i * 128 : (i + 1) * 128] = kept.T.astype(BF16)

    def make_table(pos):
        held = assign_rows_ref[...]
        held = jnp.where(iota((2, 512), 0) < counts_row_ref[...], held, 0)
        digits = jnp.concatenate([held >> 1, held & 1], axis=0).astype(F32).astype(BF16)
        place = iota((256, 1), 0)
        place = place // 2 % 8 * 64 + place % 2 * 16 + place // 16
        lane = iota((256, 512), 1)
        low = dot(jnp.where(lane == place, 1.0, 0.0).astype(BF16), digits, ((1,), (1,)))
        high = dot(jnp.where(lane == place + 32, 1.0, 0.0).astype(BF16), digits, ((1,), (1,)))
        m = 2.0 * (low[:, pos : pos + 1] + high[:, 1 - pos : 2 - pos]) + (
            low[:, 2 + pos : 3 + pos] + high[:, 3 - pos : 4 - pos]
        )
        m = m.astype(jnp.int32)
        fine = (m * iota((256, 128), 1) & 1023).astype(F32) * (2.0 * math.pi / 1024)
        scale = 1.0 / math.sqrt(512)
        cos_at = jnp.cos(fine)
        sin_at = jnp.sin(fine)
        half_cos = cos_at[:, 64:65]
        half_sin = sin_at[:, 64:65]
        cos_step = 1.0 - 2.0 * half_sin * half_sin
        sin_step = 2.0 * half_sin * half_cos
        cos_at = cos_at * scale
        sin_at = sin_at * scale
        back = jnp.where(m == 0, 0.5, 1.0)
        for k in range(8):
            re = cos_at.astype(BF16)
            im = (-sin_at).astype(BF16)
            lanes = slice(k * 128, (k + 1) * 128)
            table[pos * 512 : pos * 512 + 256, lanes] = re
            table[pos * 512 + 256 : pos * 512 + 512, lanes] = im
            table_back[pos * 512 : pos * 512 + 256, lanes] = (re.astype(F32) * back).astype(BF16)
            table_back[pos * 512 + 256 : pos * 512 + 512, lanes] = (im.astype(F32) * back).astype(BF16)
            cos_at, sin_at = cos_at * cos_step - sin_at * sin_step, sin_at * cos_step + cos_at * sin_step

    def fold(j, h):
        q = 2 * j + h
        receive(0, q)
        pairs = [xr[q, p] + xr[q, p + 2] for p in range(2)]
        if h == 0:
            for y in range(NY):
                for p in range(2):
                    ys[q, y, p] = pairs[p][:, y * 128 : (y + 1) * 128]
            send(1, q)
        else:
            rows = [pairs[p][:, y * 128 : (y + 1) * 128] for y in range(NY) for p in range(2)]
            zs[q] = by_z(turned(jnp.concatenate(rows, axis=0)))
            send(2, q)

    def middle(j, h):
        q = 2 * j + h
        if h == 0:
            receive(1, q)
            zs[q] = by_z(turned(yr[q]))
            send(2, q)
        else:
            receive(2, q)
            ys[q] = by_y(turned(zr[q]))
            send(1, q)

    def to_grid(i):
        for g in range(NG):
            for h in range(2):
                q = 2 * (NG * i + g) + h
                if h == 0:
                    receive(2, q)
                    block = zr[q].reshape(256, 128).T
                else:
                    receive(1, q)
                    block = turned(yr[q]).T
                for p in range(4):
                    row = h * 96 + g * 32
                    lhs[row : row + 32, p * 256 : (p + 1) * 256] = block[p * 32 : (p + 1) * 32]

        @pl.loop(0, 4)
        def _(b):
            lanes = pl.ds(pl.multiple_of(b * 256, 256), 256)
            fields[:, lanes] = dot(lhs[...], table[:, lanes])

    def products(i):
        row_t = (iota((8, 128), 0) * 0 + ang * NC + i).astype(F32)
        north = (row_t + 0.5) * (math.pi / 384)
        for h in range(2):
            colat = math.pi - north if h == 1 else north
            along = (coriolis * jnp.cos(colat))[0:1, 0:1]
            across = (-coriolis * jnp.sin(colat))[0:1, 0:1]
            weight = (math.pi / 2 * jnp.sin(colat))[0:1, 0:1]

            @pl.loop(0, 4)
            def _(b):
                lanes = pl.ds(pl.multiple_of(b * 256, 256), 256)
                u = [fields[h * 96 + c * 16 : h * 96 + (c + 1) * 16, lanes] for c in range(3)]
                v = [fields[h * 96 + (c + 3) * 16 : h * 96 + (c + 4) * 16, lanes] for c in range(3)]
                w = [flow[c, 2 * i + h, :, lanes].astype(F32) for c in range(3)]
                f = [mag[c, 2 * i + h, :, lanes].astype(F32) for c in range(3)]
                spin = [w[0] + along, w[1] + across, w[2]]
                for c in range(3):
                    n, o = (c + 1) % 3, (c + 2) % 3
                    momentum = (u[n] * spin[o] - u[o] * spin[n]) + (f[n] * v[o] - f[o] * v[n])
                    induction = (u[n] * f[o] - u[o] * f[n]) + (w[n] * v[o] - w[o] * v[n])
                    row = h * 96 + c * 16
                    prods[row : row + 16, lanes] = (momentum * weight).astype(BF16)
                    prods[row + 48 : row + 64, lanes] = (induction * weight).astype(BF16)

    def from_grid(i):
        @pl.loop(0, 4)
        def _(p):
            rows = pl.ds(pl.multiple_of(p * 256, 256), 256)
            returned = dot(prods[...], table_back[rows, :], ((1,), (1,)))
            returned = returned.astype(BF16).astype(F32)
            n, s = returned[:96], returned[96:]
            fields[0:96, rows] = n + s
            fields[96:192, rows] = n - s

        for g in range(NG):
            for h in range(2):
                row = h * 96 + g * 32
                block = jnp.concatenate([fields[row : row + 32, p * 256 : (p + 1) * 256] for p in range(4)], axis=0)
                block = block.T.astype(BF16)
                q = 2 * (NG * i + g) + h
                if h == 0:
                    zbs[q] = by_z(block)
                    send(3, q)
                else:
                    ybs[q] = by_y(turned(block))
                    send(4, q)

    def gather(j, h):
        q = 2 * j + h
        if h == 0:
            receive(3, q)
            ybs[q] = by_y(turned(zbr[q]))
            send(4, q)
        else:
            receive(4, q)
            zbs[q] = by_z(turned(ybr[q]))
            send(3, q)

    def unfold(j, h):
        q = 2 * j + h
        if h == 0:
            receive(4, q)
        else:
            receive(3, q)
            ybr[q] = by_y(turned(zbr[q]))
        send(5, q)

    def finish(g):
        pieces = [2 * (NG * i + g) + h for i in range(NC) for h in range(2)]
        for q in pieces:
            receive(5, q)
        parts = []
        for b in range(4):
            rows = jnp.concatenate(
                [
                    jnp.concatenate([xbr[q, :, 2 * b + e].reshape(64, 128) for q in pieces], axis=0)
                    for e in range(2)
                ],
                axis=1,
            )
            first = iota((256, 256), 1) % 128 < 64
            parts.append(jnp.where(first, dot(leg_back[0], rows), dot(leg_back[1], rows)).astype(BF16))
        nonlinear = jnp.concatenate(parts, axis=1)
        for pos in range(2):
            order, top = live_order(pos)
            n = iota((256, 128), 0)
            degree = (order + n).astype(F32)
            damping = jnp.where(n <= top, 1.0 / (1.0 + degree * (degree + 1.0) / 65536.0), 0.0)
            for x in range(2):
                j = pos * 4 + x * 2
                terms = dot(nonlinear, swap[:, j * 128 : (j + 2) * 128]).astype(BF16)
                for cc in range(2):
                    c = 2 * g + cc
                    joined = jnp.concatenate([state[c, x, slot(pos)], terms[:, cc * 128 : (cc + 1) * 128]], axis=1)
                    stepped = dot(joined, ops_ref[c // 3], ((1,), (1,)))
                    out[c, x, slot(pos)] = (stepped * damping).astype(BF16)
        stores[g].start()

    by_piece = {"fold": fold, "middle": middle, "gather": gather, "unfold": unfold}
    by_chunk = {"to_grid": to_grid, "products": products, "from_grid": from_grid}

    def late_table():
        make_table(1)
        loads[NG].wait()
        loads[NG + 1].wait()

    once = {
        "early_table": lambda: make_table(0),
        "late_table": late_table,
        "transposed_legendre": transposed_legendre,
    }

    @pl.loop(0, max(lag for _, _, lag in SCHEDULE) + NP)
    def _(step):
        for what, h, lag in SCHEDULE:
            if what in once:
                due = step == lag
            else:
                due = (step >= lag) & (step < lag + NP)
            if what in by_chunk:
                due &= (step - lag) % NG == 0

            @pl.when(due)
            def _():
                if what in once:
                    once[what]()
                elif what in by_chunk:
                    by_chunk[what]((step - lag) // NG)
                elif what == "synthesis":
                    synthesis(step - lag)
                else:
                    by_piece[what](step - lag, h)

    finish(0)
    finish(1)
    finish(2)
    for k in range(6):
        all_sent(k)
    for store in stores:
        store.wait()


def per_device(state, legendre, radial_ops, base_flow, base_field, assign, counts):
    vmem = pl.BlockSpec(memory_space=pltpu.VMEM)
    smem = pl.BlockSpec(memory_space=pltpu.SMEM)
    hbm = pl.BlockSpec(memory_space=pl.ANY)
    dma = pltpu.SemaphoreType.DMA
    assign_rows = assign.T
    return pl.pallas_call(
        kernel,
        out_shape=jax.ShapeDtypeStruct(state.shape, BF16),
        in_specs=[smem, smem, vmem, vmem, vmem, vmem, hbm, hbm, hbm],
        out_specs=hbm,
        scratch_shapes=[
            pltpu.VMEM(state.shape, BF16),
            pltpu.VMEM(base_flow.shape, BF16),
            pltpu.VMEM(base_field.shape, BF16),
            pltpu.VMEM(state.shape, BF16),
            pltpu.VMEM((1024, 1024), BF16),
            pltpu.VMEM((256, 256), BF16),
            pltpu.VMEM((NC, 256, 256), BF16),
            pltpu.VMEM((2, 256, 384), BF16),
            pltpu.VMEM((NG, 256, 1024), BF16),
            pltpu.VMEM((1024, 1024), BF16),
            pltpu.VMEM((1024, 1024), BF16),
            pltpu.VMEM((192, 1024), BF16),
            pltpu.VMEM((192, 1024), F32),
            pltpu.VMEM((192, 1024), BF16),
            pltpu.VMEM((NQ, NX, 16, 1024), BF16),
            pltpu.VMEM((NQ, NX, 16, 1024), BF16),
            pltpu.VMEM((NQ, NY, 2, 16, 128), BF16),
            pltpu.VMEM((NQ, NY, 2, 16, 128), BF16),
            pltpu.VMEM((NQ, NZ, 16, 128), BF16),
            pltpu.VMEM((NQ, NZ, 16, 128), BF16),
            pltpu.VMEM((NQ, NZ, 16, 128), BF16),
            pltpu.VMEM((NQ, NZ, 16, 128), BF16),
            pltpu.VMEM((NQ, NY, 2, 16, 128), BF16),
            pltpu.VMEM((NQ, NY, 2, 16, 128), BF16),
            pltpu.VMEM((NQ, NX, NY, 16, 128), BF16),
            dma((6,)),
            dma((6, NQ)),
            dma((6, NQ)),
            dma((NG + 2,)),
            dma((NG,)),
        ],
        compiler_params=pltpu.CompilerParams(
            collective_id=0, has_side_effects=True, vmem_limit_bytes=56 * 1024 * 1024
        ),
    )(
        assign_rows,
        counts,
        assign_rows,
        counts.reshape(1, -1),
        legendre,
        radial_ops,
        state,
        base_flow,
        base_field,
    )


def solution(mesh):
    placed = (
        P(None, None, ("rad", "ang"), None, None),
        P(("rad", "ang"), None, None),
        P(),
        P(None, "ang", "rad", None),
        P(None, "ang", "rad", None),
        P(),
        P(),
    )
    return jax.shard_map(
        per_device,
        mesh=mesh,
        in_specs=placed,
        out_specs=P(None, None, ("rad", "ang"), None, None),
        check_vma=False,
    )
```
